32 devices in a mesh: transit: 8 (over z, y), lateral: 4 (over x, core).
Axes of the slice: x: 2, y: 2, z: 4, core: 2. Of those that a mesh axis runs over, the one named last changes fastest.
Arguments:
- displacement: float32 [6, 512, 512], P(None, 'transit', 'lateral'), may hold values from -3.06 to 3.06
- velocity: float32 [6, 512, 512], P(None, 'transit', 'lateral'), may hold values from -6.3 to 6.3
- damage: float32 [512, 512], P('transit', 'lateral'), may hold values from 0 to 0.3
- strength: float32 [512, 512], P('transit', 'lateral'), may hold values from 0.3 to 3
- contact: int32 [512, 512], P('transit', 'lateral'), may hold values 0 or 1
- flaw_cells: int32 [8, 4, 32], P('transit', 'lateral'), may hold values from 0 to 8191, as said below
Outputs:
- new_displacement: float32 [6, 512, 512], P(None, 'transit', 'lateral')
- new_velocity: float32 [6, 512, 512], P(None, 'transit', 'lateral')
- new_damage: float32 [512, 512], P('transit', 'lateral')
The draws below stay inside these ranges and needn't reach their ends.
Inputs may be any that keep to these rules, and one draw needn't show every extreme that they name: `flaw_cells`: entry [t, l, j] is the node (row * 128 + column) of the tile with transit index t and lateral index l, a tile holding 64 x 128 nodes; entries may repeat.
All inputs are finite; a program needn't handle non-finite values. No bound on the sum of `contact` on one device may be relied on, other than what follows from the above.
Results may differ from the reference program's by a relative error of at most 0.0001.
Values sent between devices are 32-bit elements; how exact they have to be, the bound alone decides.
No kernel may reach another device: no remote copies, remote signals or barrier semaphores. Data moves between devices by JAX's collectives and lax.ppermute only.
A program may use at most 64 MiB of HBM per device.

```python
import math
import jax
import jax.numpy as jnp
import numpy as np
from jax import lax

CX = 64
CY = 128
STEPS = 2
RADIUS = 8
FLAWS = 32
TILES_T = 8
TILES_L = 4
NX = 512
NY = 512


def block_levels(key):
    levels = jax.random.uniform(key, (NX // 32 + 1, NY // 32 + 1), jnp.float32)
    row_idx = jnp.arange(NX, dtype=jnp.int32) // 32
    col_idx = jnp.arange(NY, dtype=jnp.int32) // 32
    return levels[row_idx][:, col_idx]


def draw_displacement(key, part):
    level = block_levels(key)
    key = jax.random.fold_in(key, 11)
    noise = jnp.clip(jax.random.normal(key, (6, NX, NY), jnp.float32), -3.0, 3.0)
    return (0.02 + level)[None, :, :] * noise


def draw_velocity(key, part):
    level = block_levels(key)
    key = jax.random.fold_in(key, 12)
    noise = jnp.clip(jax.random.normal(key, (6, NX, NY), jnp.float32), -3.0, 3.0)
    return (0.1 + 2.0 * (1.0 - level))[None, :, :] * noise


def draw_flaw_cells(key, part):
    key = jax.random.fold_in(key, 13)
    chosen = jax.random.randint(key, (TILES_T, TILES_L, FLAWS), 0, CX * CY, dtype=jnp.int32)
    chosen = chosen.at[0, 0, 0].set(CX * CY - 1)
    return chosen.at[TILES_T - 1, TILES_L - 1, 0].set(0)


def place_ends(array, stream_key, least, top_value):
    dims = array.shape
    spot = [jax.random.randint(jax.random.fold_in(stream_key, axis), (), 0, dims[axis]) for axis in range(len(dims))]
    array = array.at[tuple(spot)].set(least)
    longest = dims.index(max(dims))
    spot[longest] = (spot[longest] + 1) % dims[longest]
    return array.at[tuple(spot)].set(top_value)


def block_scale(key, shape, shards, low, high):
    loudness, own = 1.0, jax.random.fold_in(key, 6)
    for dim, parts in shards:
        heights = jnp.exp(jax.random.uniform(jax.random.fold_in(own, dim), (parts,), jnp.float32, low / len(shards), high / len(shards)))
        loudness = loudness * jnp.repeat(heights, shape[dim] // parts).reshape([-1 if axis == dim else 1 for axis in range(len(shape))])
    return loudness


def setup_inputs(seed: int = 0) -> dict:
    streams_of = jax.random.split(jax.random.key(seed), 7)
    displacement = draw_displacement(jax.random.fold_in(streams_of[6], 71), 0)
    velocity = draw_velocity(jax.random.fold_in(streams_of[6], 71), 0)
    damage = jnp.clip(0.3 * jax.random.uniform(streams_of[2], (NX, NY), jnp.float32) ** block_scale(streams_of[2], (NX, NY), ((0, 8), (1, 4)), -0.2, 0.2), 0.0, 0.3)
    strength = jnp.clip(jnp.exp(math.log(3.0) - 2.3025851 * jax.random.uniform(streams_of[3], (NX, NY), jnp.float32) ** block_scale(streams_of[3], (NX, NY), ((0, 8), (1, 4)), -0.2, 0.2)), 0.3, 3.0)
    contact = place_ends((jax.random.randint(streams_of[4], (NX, NY), 0, 8) < 1).astype(jnp.int32), jax.random.fold_in(streams_of[4], 1), 0, 1)
    flaw_cells = draw_flaw_cells(jax.random.fold_in(streams_of[6], 71), 0)
    return {"displacement": displacement, "velocity": velocity, "damage": damage, "strength": strength, "contact": contact, "flaw_cells": flaw_cells}


lap_stiffness = (1.0, 1.0, 0.0, 0.5, 0.5, 0.2)
viscous_coef = 0.2
along_pairs = ((2, 3, 1.0, 0.8), (1, 5, 1.0, 0.3))
across_pairs = ((2, 4, 1.0, 0.8), (0, 5, -1.0, 0.3))
contact_stiff = 2.0
hull_goal = (1.5, 0.0, -0.5, 0.0, 0.0, 0.0)
hull_select = (1.0, 0.0, 1.0, 0.0, 0.0, 0.0)
time_step = 0.4
keep_rate = 0.95
flaw_weaken = 0.6
soften_scale = 6.0
spread_denominator = 32.0
fibre_depth = (-0.75, -0.25, 0.25, 0.75)
channel_threshold = (0.6, 0.6, 1.2, 0.6, 0.6, 1.2, 0.6, 0.6, 1.2, 0.6, 0.6, 1.2, 1.5, 1.5, 1.2, 1.0)


def channel_table():
    coef_table = np.zeros((16, 9), np.float32)
    for fibre_idx in range(4):
        for component in range(3):
            coef_table[3 * fibre_idx + component, component] = 1.0
            coef_table[3 * fibre_idx + component, 3 + component] = fibre_depth[fibre_idx]
    coef_table[12, 6] = 1.0
    coef_table[13, 7] = 1.0
    coef_table[14, 8] = 1.0
    coef_table[15, 5] = 1.0
    return jnp.asarray(coef_table)


def neighbours(padded):
    return (padded[..., 2:, 1:-1], padded[..., :-2, 1:-1], padded[..., 1:-1, 2:], padded[..., 1:-1, :-2])


def strain_fields(middle, beside_all):
    plus_x, minus_x, plus_y, minus_y = beside_all
    slope_x = 0.5 * (plus_x - minus_x)
    slope_y = 0.5 * (plus_y - minus_y)
    return jnp.stack([
        slope_x[0], slope_y[1], slope_y[0] + slope_x[1],
        slope_x[3], slope_y[4], slope_y[3] + slope_x[4],
        slope_x[2] - middle[3], slope_y[2] - middle[4],
        0.5 * (slope_x[1] - slope_y[0]) - middle[5]])


def edge_force(middle, other, sense, pairs):
    change = other - middle
    pieces = [lap_stiffness[comp_idx] * change[comp_idx] + viscous_coef * change[6 + comp_idx] for comp_idx in range(6)]
    for lead_comp, turn_comp, sign_lead, stiff_coef in pairs:
        shear_term = sign_lead * sense * change[lead_comp] - 0.5 * (middle[turn_comp] + other[turn_comp])
        pieces[lead_comp] = pieces[lead_comp] + sense * sign_lead * stiff_coef * shear_term
        pieces[turn_comp] = pieces[turn_comp] + 0.5 * stiff_coef * shear_term
    return jnp.stack(pieces)


def smooth_axis(field, axis_pos, taps):
    extent = field.shape[axis_pos]
    widths = [(0, 0), (0, 0)]
    widths[axis_pos] = (RADIUS, RADIUS)
    padded = jnp.pad(field, widths)
    total = jnp.zeros_like(field)
    for shift_idx in range(2 * RADIUS + 1):
        total = total + taps[shift_idx] * lax.slice_in_dim(padded, shift_idx, shift_idx + extent, axis=axis_pos)
    return total


def reference(displacement, velocity, damage, strength, contact, flaw_cells):
    offsets = (jnp.arange(2 * RADIUS + 1, dtype=jnp.int32) - RADIUS).astype(jnp.float32)
    taps = jnp.exp(-offsets * offsets / spread_denominator)
    ones_grid = jnp.ones((NX, NY), jnp.float32)
    coverage = smooth_axis(smooth_axis(ones_grid, 0, taps), 1, taps)
    row_base = (jnp.arange(TILES_T, dtype=jnp.int32) * CX)[:, None, None]
    col_base = (jnp.arange(TILES_L, dtype=jnp.int32) * CY)[None, :, None]
    rows_at = (row_base + flaw_cells // CY).reshape(-1).astype(jnp.int32)
    cols_at = (col_base + flaw_cells % CY).reshape(-1).astype(jnp.int32)
    flawed = jnp.zeros((NX, NY), jnp.float32).at[rows_at, cols_at].set(1.0)
    limit = strength * (1.0 - flaw_weaken * flawed)
    grip = contact.astype(jnp.float32) * contact_stiff
    goal = jnp.asarray(hull_goal, jnp.float32)[:, None, None]
    select = jnp.asarray(hull_select, jnp.float32)[:, None, None]
    coef_table = channel_table()
    thresholds = jnp.asarray(channel_threshold, jnp.float32)
    edge_senses = (1.0, -1.0, 1.0, -1.0)
    edge_pairs = (along_pairs, along_pairs, across_pairs, across_pairs)
    for step_idx in range(STEPS):
        state_now = jnp.concatenate([displacement, velocity], 0)
        padded = jnp.pad(state_now, ((0, 0), (1, 1), (1, 1)))
        middle = padded[:, 1:-1, 1:-1]
        beside_all = neighbours(padded)
        fields = strain_fields(middle[:6], tuple(piece[:6] for piece in beside_all))

        def add_channel(driving, row):
            coef_row, threshold = row
            energy = jnp.tensordot(coef_row, fields, axes=1, precision=lax.Precision.HIGHEST) ** 2
            averaged = smooth_axis(smooth_axis(energy, 0, taps), 1, taps) / coverage
            return driving + jnp.maximum(averaged - limit * threshold, 0.0), None

        driving, unused = lax.scan(add_channel, jnp.zeros((NX, NY), jnp.float32), (coef_table, thresholds))
        damage = jnp.maximum(damage, 1.0 - jnp.exp(-driving / soften_scale))
        damage_near = neighbours(jnp.pad(damage, 1))
        force = jnp.zeros_like(displacement)
        for piece, sense, pairs, near in zip(beside_all, edge_senses, edge_pairs, damage_near):
            force = force + (1.0 - 0.5 * (damage + near)) * edge_force(middle, piece, sense, pairs)
        force = force + grip * select * (goal - displacement)
        velocity = keep_rate * velocity + time_step * force
        displacement = displacement + time_step * velocity
    return displacement, velocity, damage
```

```python
import functools

import jax
import jax.numpy as jnp
from jax import lax
from jax.experimental import pallas as pl
from jax.experimental.pallas import tpu as pltpu
from jax.sharding import PartitionSpec as P

RADIUS = 8
CX, CY = 64, 128
WIDE, NEAR = 20, 11
PAD = 24
ROWS = CX + 2 * PAD
OFF = 8
HELD = ROWS + 2 * OFF
LANES = 128
SLAB = 224
K_STIFF = (1.0, 1.0, 0.0, 0.5, 0.5, 0.2)
VISCOUS = 0.2
KEEP = 0.95
DT = 0.4
ALONG = ((2, 3, 1.0, 0.8), (1, 5, 1.0, 0.3))
ACROSS = ((2, 4, 1.0, 0.8), (0, 5, -1.0, 0.3))
STEP_ROWS = ((0, 112, 8, 104, 8, 104), (8, 104, 16, 96, 24, 88))
F32, BF16 = jnp.float32, jnp.bfloat16


def halo_of(field):
    return WIDE if field < 6 else NEAR


def slab_start(field):
    return WIDE * field if field < 6 else 6 * WIDE + NEAR * (field - 6)


def swap(block, axis):
    count = lax.axis_size(axis)
    out = []
    for first, part in zip((0, 1), block):
        pairs = []
        for i in range(first, count - 1, 2):
            pairs += [(i, i + 1), (i + 1, i)]
        out.append(lax.ppermute(part, axis, pairs))
    return out


def pack_kernel(flaw, disp, vel, dam, stren, con, out_a, out_b, lim):
    node = lax.broadcasted_iota(jnp.int32, (CX, CY), 0) * CY + lax.broadcasted_iota(
        jnp.int32, (CX, CY), 1
    )
    mark = node == flaw[0, 0, 0]
    for j in range(1, flaw.shape[2]):
        mark = mark | (node == flaw[0, 0, j])
    lim[...] = stren[...] * jnp.where(mark, 0.4, 1.0)

    def field(k, rows):
        if k < 6:
            return disp[k, rows, :]
        if k < 12:
            return vel[k - 6, rows, :]
        if k == 12:
            return dam[rows, :]
        if k == 13:
            return lim[rows, :]
        return con[rows, :].astype(F32)

    def fill(out, top):
        for k in range(15):
            width = halo_of(k)
            rows = slice(0, width) if top else slice(CX - width, CX)
            start = slab_start(k)
            out[start : start + width, :] = field(k, rows)
        out[219:SLAB, :] = jnp.zeros((SLAB - 219, LANES), F32)

    even = lax.rem(lax.axis_index("transit"), 2) == 0

    @pl.when(even)
    def _():
        fill(out_a, False)
        fill(out_b, True)

    @pl.when(jnp.logical_not(even))
    def _():
        fill(out_a, True)
        fill(out_b, False)


def assemble(ext, disp, vel, dam, lim, con, got_a, got_b):
    even = lax.rem(lax.axis_index("transit"), 2) == 0
    for k in range(15):
        width, start = halo_of(k), slab_start(k)
        part_a = got_a[start : start + width, :]
        part_b = got_b[start : start + width, :]
        if k < 6:
            own = disp[k]
        elif k < 12:
            own = vel[k - 6]
        else:
            own = (dam, lim, con)[k - 12][...].astype(F32)
        low, high = OFF + PAD, OFF + PAD + CX
        ext[k, 0 : low - width, :] = jnp.zeros((low - width, LANES), F32)
        ext[k, low - width : low, :] = jnp.where(even, part_b, part_a)
        ext[k, low:high, :] = own
        ext[k, high : high + width, :] = jnp.where(even, part_a, part_b)
        ext[k, high + width : HELD, :] = jnp.zeros((HELD - high - width, LANES), F32)


def edge_kernel(disp, vel, dam, lim, con, got_a, got_b, out_a, out_b, ext):
    assemble(ext, disp, vel, dam, lim, con, got_a, got_b)
    lane = lax.broadcasted_iota(jnp.int32, (ROWS, LANES), 1)
    even = lax.rem(lax.axis_index("lateral"), 2) == 0
    for tile, fields in ((0, range(6)), (1, range(6, 15))):
        right = left = jnp.zeros((ROWS, LANES), F32)
        for n, k in enumerate(fields):
            width = halo_of(k)
            here = (lane >= n * width) & (lane < (n + 1) * width)
            block = ext[k, OFF : OFF + ROWS, :]
            right = jnp.where(here, pltpu.roll(block, (n * width - (CY - width)) % LANES, 1), right)
            left = jnp.where(here, pltpu.roll(block, n * width, 1) if n else block, left)
        cols = slice(tile * LANES, (tile + 1) * LANES)
        out_a[:, cols] = jnp.where(even, right, left)
        out_b[:, cols] = jnp.where(even, left, right)


def split(x):
    high = x.astype(BF16)
    return high, (x - high.astype(F32)).astype(BF16)


def step_kernel(
    disp, vel, dam, lim, con, got_a, got_b, side_a, side_b,
    along_1, along_2, across_hi, across_lo, cover, decay, rate,
    out_u, out_v, out_d,
    ext, ext2, mid, wp, fm, hd, energy, t_hi, t_lo, aver,
):
    assemble(ext.at[0], disp, vel, dam, lim, con, got_a, got_b)
    lane8 = lax.broadcasted_iota(jnp.int32, (8, LANES), 1)
    lane = lax.broadcasted_iota(jnp.int32, (ROWS, LANES), 1)
    even = lax.rem(lax.axis_index("lateral"), 2) == 0
    for tile, fields in ((0, range(6)), (1, range(6, 15))):
        cols = slice(tile * LANES, (tile + 1) * LANES)
        right = jnp.where(even, side_a[:, cols], side_b[:, cols])
        left = jnp.where(even, side_b[:, cols], side_a[:, cols])
        for n, k in enumerate(fields):
            width = halo_of(k)
            from_right = pltpu.roll(right, (-n * width) % LANES, 1) if n else right
            from_left = pltpu.roll(left, (CY - width - n * width) % LANES, 1)
            ext[1, k, 0:OFF, :] = jnp.zeros((OFF, LANES), F32)
            ext[1, k, OFF : OFF + ROWS, :] = jnp.where(lane < 64, from_right, from_left)
            ext[1, k, OFF + ROWS : HELD, :] = jnp.zeros((OFF, LANES), F32)
    for tile in range(2):
        for k in range(12):
            for low in (0, OFF + 104):
                ext2[tile, k, low : low + 16, :] = jnp.zeros((16, LANES), F32)
        for low in (0, HELD - 16):
            hd[tile, low : low + 16, :] = jnp.full((16, LANES), 0.5, F32)

    def after(pair):
        last = lax.broadcasted_iota(jnp.int32, pair[0].shape, 1) == LANES - 1
        r0, r1 = (pltpu.roll(x, LANES - 1, 1) for x in pair)
        return jnp.where(last, r1, r0), jnp.where(last, r0, r1)

    def before(pair):
        first = lax.broadcasted_iota(jnp.int32, pair[0].shape, 1) == 0
        r0, r1 = (pltpu.roll(x, 1, 1) for x in pair)
        return jnp.where(first, r1, r0), jnp.where(first, r0, r1)

    state, after_state = ext, ext2
    for step, (e0, e1, d0, d1, f0, f1) in enumerate(STEP_ROWS):
        last_step = step == 1
        span = e1 - e0
        for b in range(e0, e1, 16):
            def rows(k, shift=0):
                return tuple(state[tile, k, OFF + b + shift : OFF + b + shift + 16, :] for tile in range(2))
            here = [rows(k) for k in range(6)]
            dx = [tuple(p - m for p, m in zip(rows(k, 1), rows(k, -1))) for k in range(5)]
            dy = [tuple(p - m for p, m in zip(after(here[k]), before(here[k]))) for k in range(5)]
            for tile in range(2):
                x = [v[tile] for v in dx]
                y = [v[tile] for v in dy]
                c = [v[tile] for v in here]
                plane = (x[0], y[1], y[0] + x[1])
                bend = (x[3], y[4], y[3] + x[4])
                e7 = x[2] - 2.0 * c[3]
                e8 = y[2] - 2.0 * c[4]
                e9 = 0.5 * (x[1] - y[0]) - 2.0 * c[5]
                prods = []
                for p, q in zip(plane, bend):
                    prods += [p * p, p * q, q * q]
                prods += [e7 * e7, e8 * e8, e9 * e9]
                for ch, value in enumerate(prods):
                    high, low = split(value)
                    cols = slice(tile * LANES, (tile + 1) * LANES)
                    energy[ch, b - e0 : b - e0 + 16, cols] = high
                    energy[ch, span + b - e0 : span + b - e0 + 16, cols] = low
        band = along_2 if last_step else along_1
        n_out = d1 - d0
        for ch in range(12):
            both = jnp.dot(band[...], energy[ch, 0 : 2 * span, :], preferred_element_type=F32)
            high, low = split(both[:n_out] + both[n_out:])
            t_hi[ch * n_out : (ch + 1) * n_out, :] = high
            t_lo[ch * n_out : (ch + 1) * n_out, :] = low
        total = 12 * n_out
        aver[0:total, :] = (
            jnp.dot(t_hi[0:total, :], across_hi[...], preferred_element_type=F32)
            + jnp.dot(t_lo[0:total, :], across_hi[...], preferred_element_type=F32)
            + jnp.dot(t_hi[0:total, :], across_lo[...], preferred_element_type=F32)
        )
        for b in range(d0, d1, 8):
            for tile in range(2):
                cols = slice(tile * LANES, (tile + 1) * LANES)
                at = slice(OFF + b, OFF + b + 8)
                def mean(ch):
                    start = ch * n_out + b - d0
                    return aver[start : start + 8, cols]
                level = state[tile, 13, at, :] if step == 0 else ext[tile, 13, at, :]
                level = level * cover[b : b + 8, cols]
                driving = jnp.zeros((8, LANES), F32)
                for comp, threshold in enumerate((0.6, 0.6, 1.2)):
                    p, q, r = (mean(3 * comp + n) for n in range(3))
                    base = p - threshold * level
                    for depth in (0.75, 0.25):
                        centre = base + (depth * depth) * r
                        swing = (2.0 * depth) * q
                        driving += jnp.maximum(centre + swing, 0.0) + jnp.maximum(centre - swing, 0.0)
                    if comp == 2:
                        driving += jnp.maximum(r - level, 0.0)
                for ch, threshold in ((9, 1.5), (10, 1.5), (11, 1.2)):
                    driving += jnp.maximum(mean(ch) - threshold * level, 0.0)
                new = jnp.maximum(
                    ext[tile, 12, at, :], 1.0 - jnp.exp(driving * decay[b : b + 8, cols])
                )
                ext[tile, 12, at, :] = new
                hd[tile, at, :] = 0.5 - 0.5 * new
                if last_step and tile == 0 and PAD <= b < PAD + CX:
                    out_d[b - PAD : b - PAD + 8, :] = new
        for b in range(f0 - 8, f1 + 8, 8):
            at = slice(OFF + b, OFF + b + 8)
            for tile in range(2):
                u = [state[tile, k, at, :] for k in range(6)]
                v = [state[tile, 6 + k, at, :] for k in range(6)]
                for k in range(6):
                    value = VISCOUS * v[k]
                    if K_STIFF[k] == 1.0:
                        value = u[k] + value
                    elif K_STIFF[k]:
                        value = K_STIFF[k] * u[k] + value
                    wp[tile, k, at, :] = value
                for n, (lead, turn, sign, _) in enumerate(ALONG):
                    wp[tile, 6 + n, at, :] = sign * u[lead] - 0.5 * u[turn]
        for b in range(f0 - 8, f1, 8):
            at = slice(OFF + b, OFF + b + 8)
            nxt = slice(OFF + b + 1, OFF + b + 9)
            prv = slice(OFF + b - 1, OFF + b + 7)

            def fluxes(base, gammas, s, pairs):
                plus, minus = list(base), list(base)
                for gamma, (lead, turn, sign, stiff) in zip(gammas, pairs):
                    plus[lead] = minus[lead] = base[lead] + (sign * stiff) * gamma
                    half = (0.5 * stiff) * gamma
                    plus[turn], minus[turn] = base[turn] + half, base[turn] - half
                out_p = [s * x for x in plus]
                out_m = [out_p[k] if plus[k] is minus[k] else s * minus[k] for k in range(6)]
                return out_p, out_m

            force = [None, None]
            for tile in range(2):
                if last_step and tile == 1:
                    continue
                u = {k: state[tile, k, at, :] for k in (1, 2, 3, 5)}
                base = [wp[tile, k, nxt, :] - wp[tile, k, at, :] for k in range(6)]
                gammas = [
                    wp[tile, 6 + n, nxt, :] - (sign * u[lead] + 0.5 * u[turn])
                    for n, (lead, turn, sign, _) in enumerate(ALONG)
                ]
                s = hd[tile, at, :] + hd[tile, nxt, :]
                plus, minus = fluxes(base, gammas, s, ALONG)
                for k in range(6):
                    fm[tile, k, at, :] = minus[k]
                if b >= f0:
                    force[tile] = [plus[k] - fm[tile, k, prv, :] for k in range(6)]
            if b < f0:
                continue
            u = [[state[tile, k, at, :] for k in range(6)] for tile in range(2)]
            w = [[wp[tile, k, at, :] for k in range(6)] for tile in range(2)]
            w_next = [after((w[0][k], w[1][k])) for k in range(6)]
            p_next = [
                after(tuple(sign * u[tile][lead] - 0.5 * u[tile][turn] for tile in range(2)))
                for lead, turn, sign, _ in ACROSS
            ]
            h = tuple(hd[tile, at, :] for tile in range(2))
            h_next = after(h)
            plus, minus = [], []
            for tile in range(2):
                base = [w_next[k][tile] - w[tile][k] for k in range(6)]
                gammas = [
                    p_next[n][tile] - (sign * u[tile][lead] + 0.5 * u[tile][turn])
                    for n, (lead, turn, sign, _) in enumerate(ACROSS)
                ]
                one_p, one_m = fluxes(base, gammas, h[tile] + h_next[tile], ACROSS)
                plus.append(one_p)
                minus.append(one_m)
            minus_prev = [before((minus[0][k], minus[1][k])) for k in range(6)]
            for tile in range(2):
                if last_step and tile == 1:
                    continue
                cols = slice(tile * LANES, (tile + 1) * LANES)
                dt = rate[b : b + 8, cols]
                total = [force[tile][k] + plus[tile][k] - minus_prev[k][tile] for k in range(6)]
                grip = 2.0 * ext[tile, 14, at, :]
                total[0] = total[0] + grip * (1.5 - u[tile][0])
                total[2] = total[2] + grip * (-0.5 - u[tile][2])
                for k in range(6):
                    v_new = KEEP * state[tile, 6 + k, at, :] + dt * total[k]
                    u_new = u[tile][k] + dt * v_new
                    if last_step:
                        out_v[k, b - PAD : b - PAD + 8, :] = v_new
                        out_u[k, b - PAD : b - PAD + 8, :] = u_new
                    else:
                        after_state[tile, 6 + k, at, :] = v_new
                        after_state[tile, k, at, :] = u_new
        state = ext2


def tables(count_x, count_y):
    pos_x = jnp.arange(ROWS) + lax.axis_index("transit") * CX - PAD
    in_x = (pos_x >= 0) & (pos_x < count_x)
    ring = jnp.arange(2 * LANES)
    pos_y = lax.axis_index("lateral") * CY + jnp.where(ring < 192, ring, ring - 2 * LANES)
    in_y = (pos_y >= 0) & (pos_y < count_y)

    def weight(offset, inside):
        dist = offset.astype(F32)
        return jnp.where((jnp.abs(offset) <= RADIUS) & inside, jnp.exp(-dist * dist / 32.0), 0.0)

    row = jnp.arange(ROWS)
    along = weight(row[None, :] - row[:, None], in_x[None, :])
    across = weight((ring[:, None] - ring[None, :] + LANES) % (2 * LANES) - LANES, in_y[:, None])
    cover = jnp.sum(along, 1)[:, None] * jnp.sum(across, 0)[None, :]
    inside = in_x[:, None] & in_y[None, :]
    cover = jnp.where(inside, cover, 1.0)
    decay = jnp.where(inside, -1.0 / (24.0 * cover), 0.0)
    rate = jnp.where(inside, DT, 0.0)

    def parts(x):
        high = lax.reduce_precision(x, 8, 7)
        return high.astype(BF16), (x - high).astype(BF16)

    bands = []
    for e0, e1, d0, d1, _, _ in STEP_ROWS:
        high, low = parts(along[d0:d1, e0:e1])
        bands.append(jnp.concatenate([jnp.concatenate([high, high], 1), jnp.concatenate([low, low], 1)], 0))
    high, low = parts(across)
    return bands + [high, low, 4.0 * cover, decay, rate]


def vmem(n):
    return [pl.BlockSpec(memory_space=pltpu.VMEM)] * n


def on_device(displacement, velocity, damage, strength, contact, flaw_cells):
    params = pltpu.CompilerParams(vmem_limit_bytes=48 * 1024 * 1024)
    shape = jax.ShapeDtypeStruct
    send_a, send_b, limit = pl.pallas_call(
        pack_kernel,
        out_shape=[shape((SLAB, LANES), F32)] * 2 + [shape((CX, CY), F32)],
        in_specs=[pl.BlockSpec(memory_space=pltpu.SMEM)] + vmem(5),
        out_specs=vmem(3),
        compiler_params=params,
        name="pack_rows",
    )(flaw_cells, displacement, velocity, damage, strength, contact)
    got = swap((send_a, send_b), "transit")
    own = (displacement, velocity, damage, limit, contact)
    side = pl.pallas_call(
        edge_kernel,
        out_shape=[shape((ROWS, 2 * LANES), F32)] * 2,
        in_specs=vmem(7),
        out_specs=vmem(2),
        scratch_shapes=[pltpu.VMEM((15, HELD, LANES), F32)],
        compiler_params=params,
        name="pack_columns",
    )(*own, *got)
    side = swap(side, "lateral")
    table = tables(CX * lax.axis_size("transit"), CY * lax.axis_size("lateral"))
    out = pl.pallas_call(
        step_kernel,
        out_shape=[shape((6, CX, CY), F32)] * 2 + [shape((CX, CY), F32)],
        in_specs=vmem(16),
        out_specs=vmem(3),
        scratch_shapes=[
            pltpu.VMEM((2, 15, HELD, LANES), F32),
            pltpu.VMEM((2, 12, HELD, LANES), F32),
            pltpu.VMEM((8, LANES), F32),
            pltpu.VMEM((2, 8, HELD, LANES), F32),
            pltpu.VMEM((2, 6, HELD, LANES), F32),
            pltpu.VMEM((2, HELD, LANES), F32),
            pltpu.VMEM((12, 2 * ROWS, 2 * LANES), BF16),
            pltpu.VMEM((12 * 96, 2 * LANES), BF16),
            pltpu.VMEM((12 * 96, 2 * LANES), BF16),
            pltpu.VMEM((12 * 96, 2 * LANES), F32),
        ],
        compiler_params=params,
        name="two_steps",
    )(*own, *got, *side, *table)
    return tuple(out)


def solution(mesh):
    return jax.shard_map(
        on_device,
        mesh=mesh,
        in_specs=(
            P(None, "transit", "lateral"),
            P(None, "transit", "lateral"),
            P("transit", "lateral"),
            P("transit", "lateral"),
            P("transit", "lateral"),
            P("transit", "lateral", None),
        ),
        out_specs=(
            P(None, "transit", "lateral"),
            P(None, "transit", "lateral"),
            P("transit", "lateral"),
        ),
        check_vma=False,
    )
```

```python
import functools

import jax
import jax.numpy as jnp
from jax import lax
from jax.experimental import pallas as pl
from jax.experimental.pallas import tpu as pltpu
from jax.sharding import PartitionSpec as P

RADIUS = 8
CX, CY = 64, 128
WIDE, NEAR = 20, 11
PAD = 24
ROWS = CX + 2 * PAD
OFF = 8
HELD = ROWS + 2 * OFF
LANES = 128
SLAB = 224
K_STIFF = (1.0, 1.0, 0.0, 0.5, 0.5, 0.2)
VISCOUS = 0.2
KEEP = 0.95
DT = 0.4
ALONG = ((2, 3, 1.0, 0.8), (1, 5, 1.0, 0.3))
ACROSS = ((2, 4, 1.0, 0.8), (0, 5, -1.0, 0.3))
STEP_ROWS = ((0, 112, 8, 104, 8, 104), (8, 104, 16, 96, 24, 88))
F32, BF16 = jnp.float32, jnp.bfloat16


def halo_of(field):
    return WIDE if field < 6 else NEAR


def slab_start(field):
    return WIDE * field if field < 6 else 6 * WIDE + NEAR * (field - 6)


def swap(block, axis):
    count = lax.axis_size(axis)
    out = []
    for first, part in zip((0, 1), block):
        pairs = []
        for i in range(first, count - 1, 2):
            pairs += [(i, i + 1), (i + 1, i)]
        out.append(lax.ppermute(part, axis, pairs))
    return out


def pack_kernel(
    flaw_in, disp_in, vel_in, dam_in, stren_in, con_in,
    out_a, out_b, disp, vel, dam, lim, con, stren, flaw, sems,
):
    sources = (flaw_in, disp_in, vel_in, dam_in, stren_in, con_in)
    copies = [
        pltpu.make_async_copy(src, dst, sems.at[n])
        for n, (src, dst) in enumerate(zip(sources, (flaw, disp, vel, dam, stren, con)))
    ]
    for copy in copies:
        copy.start()
    for copy in copies:
        copy.wait()
    node = lax.broadcasted_iota(jnp.int32, (CX, CY), 0) * CY + lax.broadcasted_iota(
        jnp.int32, (CX, CY), 1
    )
    mark = node == flaw[0, 0, 0]
    for j in range(1, flaw.shape[2]):
        mark = mark | (node == flaw[0, 0, j])
    lim[...] = stren[...] * jnp.where(mark, 0.4, 1.0)

    def field(k, rows):
        if k < 6:
            return disp[k, rows, :]
        if k < 12:
            return vel[k - 6, rows, :]
        if k == 12:
            return dam[rows, :]
        if k == 13:
            return lim[rows, :]
        return con[rows, :].astype(F32)

    def fill(out, top):
        for k in range(15):
            width = halo_of(k)
            rows = slice(0, width) if top else slice(CX - width, CX)
            start = slab_start(k)
            out[start : start + width, :] = field(k, rows)
        out[219:SLAB, :] = jnp.zeros((SLAB - 219, LANES), F32)

    even = lax.rem(lax.axis_index("transit"), 2) == 0

    @pl.when(even)
    def _():
        fill(out_a, False)
        fill(out_b, True)

    @pl.when(jnp.logical_not(even))
    def _():
        fill(out_a, True)
        fill(out_b, False)


def assemble(ext, disp, vel, dam, lim, con, got_a, got_b):
    even = lax.rem(lax.axis_index("transit"), 2) == 0
    for k in range(15):
        width, start = halo_of(k), slab_start(k)
        part_a = got_a[start : start + width, :]
        part_b = got_b[start : start + width, :]
        if k < 6:
            own = disp[k]
        elif k < 12:
            own = vel[k - 6]
        else:
            own = (dam, lim, con)[k - 12][...].astype(F32)
        low, high = OFF + PAD, OFF + PAD + CX
        ext[k, 0 : low - width, :] = jnp.zeros((low - width, LANES), F32)
        ext[k, low - width : low, :] = jnp.where(even, part_b, part_a)
        ext[k, low:high, :] = own
        ext[k, high : high + width, :] = jnp.where(even, part_a, part_b)
        ext[k, high + width : HELD, :] = jnp.zeros((HELD - high - width, LANES), F32)


def edge_kernel(disp, vel, dam, lim, con, got_a, got_b, out_a, out_b, ext):
    assemble(ext, disp, vel, dam, lim, con, got_a, got_b)
    lane = lax.broadcasted_iota(jnp.int32, (ROWS, LANES), 1)
    even = lax.rem(lax.axis_index("lateral"), 2) == 0
    for tile, fields in ((0, range(6)), (1, range(6, 15))):
        right = left = jnp.zeros((ROWS, LANES), F32)
        for n, k in enumerate(fields):
            width = halo_of(k)
            here = (lane >= n * width) & (lane < (n + 1) * width)
            block = ext[k, OFF : OFF + ROWS, :]
            right = jnp.where(here, pltpu.roll(block, (n * width - (CY - width)) % LANES, 1), right)
            left = jnp.where(here, pltpu.roll(block, n * width, 1) if n else block, left)
        cols = slice(tile * LANES, (tile + 1) * LANES)
        out_a[:, cols] = jnp.where(even, right, left)
        out_b[:, cols] = jnp.where(even, left, right)


def split(x):
    high = x.astype(BF16)
    return high, (x - high.astype(F32)).astype(BF16)


def step_kernel(
    disp, vel, dam, lim, con, got_a, got_b, side_a, side_b,
    along_1, along_2, across_hi, across_lo, cover, decay, rate,
    out_u, out_v, out_d,
    ext, ext2, mid, wp, fm, hd, energy, t_hi, t_lo, aver,
):
    assemble(ext.at[0], disp, vel, dam, lim, con, got_a, got_b)
    lane8 = lax.broadcasted_iota(jnp.int32, (8, LANES), 1)
    lane = lax.broadcasted_iota(jnp.int32, (ROWS, LANES), 1)
    even = lax.rem(lax.axis_index("lateral"), 2) == 0
    for tile, fields in ((0, range(6)), (1, range(6, 15))):
        cols = slice(tile * LANES, (tile + 1) * LANES)
        right = jnp.where(even, side_a[:, cols], side_b[:, cols])
        left = jnp.where(even, side_b[:, cols], side_a[:, cols])
        for n, k in enumerate(fields):
            width = halo_of(k)
            from_right = pltpu.roll(right, (-n * width) % LANES, 1) if n else right
            from_left = pltpu.roll(left, (CY - width - n * width) % LANES, 1)
            ext[1, k, 0:OFF, :] = jnp.zeros((OFF, LANES), F32)
            ext[1, k, OFF : OFF + ROWS, :] = jnp.where(lane < 64, from_right, from_left)
            ext[1, k, OFF + ROWS : HELD, :] = jnp.zeros((OFF, LANES), F32)
    for tile in range(2):
        for k in range(12):
            for low in (0, OFF + 104):
                ext2[tile, k, low : low + 16, :] = jnp.zeros((16, LANES), F32)
        for low in (0, HELD - 16):
            hd[tile, low : low + 16, :] = jnp.full((16, LANES), 0.5, F32)

    def after(pair):
        last = lax.broadcasted_iota(jnp.int32, pair[0].shape, 1) == LANES - 1
        r0, r1 = (pltpu.roll(x, LANES - 1, 1) for x in pair)
        return jnp.where(last, r1, r0), jnp.where(last, r0, r1)

    def before(pair):
        first = lax.broadcasted_iota(jnp.int32, pair[0].shape, 1) == 0
        r0, r1 = (pltpu.roll(x, 1, 1) for x in pair)
        return jnp.where(first, r1, r0), jnp.where(first, r0, r1)

    state, after_state = ext, ext2
    for step, (e0, e1, d0, d1, f0, f1) in enumerate(STEP_ROWS):
        last_step = step == 1
        span = e1 - e0
        for b in range(e0, e1, 16):
            def rows(k, shift=0):
                return tuple(state[tile, k, OFF + b + shift : OFF + b + shift + 16, :] for tile in range(2))
            here = [rows(k) for k in range(6)]
            dx = [tuple(p - m for p, m in zip(rows(k, 1), rows(k, -1))) for k in range(5)]
            dy = [tuple(p - m for p, m in zip(after(here[k]), before(here[k]))) for k in range(5)]
            for tile in range(2):
                x = [v[tile] for v in dx]
                y = [v[tile] for v in dy]
                c = [v[tile] for v in here]
                plane = (x[0], y[1], y[0] + x[1])
                bend = (x[3], y[4], y[3] + x[4])
                e7 = x[2] - 2.0 * c[3]
                e8 = y[2] - 2.0 * c[4]
                e9 = 0.5 * (x[1] - y[0]) - 2.0 * c[5]
                prods = []
                for p, q in zip(plane, bend):
                    prods += [p * p, p * q, q * q]
                prods += [e7 * e7, e8 * e8, e9 * e9]
                for ch, value in enumerate(prods):
                    high, low = split(value)
                    cols = slice(tile * LANES, (tile + 1) * LANES)
                    energy[ch, b - e0 : b - e0 + 16, cols] = high
                    energy[ch, span + b - e0 : span + b - e0 + 16, cols] = low
        band = along_2 if last_step else along_1
        n_out = d1 - d0
        for ch in range(12):
            both = jnp.dot(band[...], energy[ch, 0 : 2 * span, :], preferred_element_type=F32)
            high, low = split(both[:n_out] + both[n_out:])
            t_hi[ch * n_out : (ch + 1) * n_out, :] = high
            t_lo[ch * n_out : (ch + 1) * n_out, :] = low
        total = 12 * n_out
        aver[0:total, :] = (
            jnp.dot(t_hi[0:total, :], across_hi[...], preferred_element_type=F32)
            + jnp.dot(t_lo[0:total, :], across_hi[...], preferred_element_type=F32)
            + jnp.dot(t_hi[0:total, :], across_lo[...], preferred_element_type=F32)
        )
        for b in range(d0, d1, 8):
            for tile in range(2):
                cols = slice(tile * LANES, (tile + 1) * LANES)
                at = slice(OFF + b, OFF + b + 8)
                def mean(ch):
                    start = ch * n_out + b - d0
                    return aver[start : start + 8, cols]
                level = state[tile, 13, at, :] if step == 0 else ext[tile, 13, at, :]
                level = level * cover[b : b + 8, cols]
                driving = jnp.zeros((8, LANES), F32)
                for comp, threshold in enumerate((0.6, 0.6, 1.2)):
                    p, q, r = (mean(3 * comp + n) for n in range(3))
                    base = p - threshold * level
                    for depth in (0.75, 0.25):
                        centre = base + (depth * depth) * r
                        swing = (2.0 * depth) * q
                        driving += jnp.maximum(centre + swing, 0.0) + jnp.maximum(centre - swing, 0.0)
                    if comp == 2:
                        driving += jnp.maximum(r - level, 0.0)
                for ch, threshold in ((9, 1.5), (10, 1.5), (11, 1.2)):
                    driving += jnp.maximum(mean(ch) - threshold * level, 0.0)
                new = jnp.maximum(
                    ext[tile, 12, at, :], 1.0 - jnp.exp(driving * decay[b : b + 8, cols])
                )
                ext[tile, 12, at, :] = new
                hd[tile, at, :] = 0.5 - 0.5 * new
                if last_step and tile == 0 and PAD <= b < PAD + CX:
                    out_d[b - PAD : b - PAD + 8, :] = new
        for b in range(f0 - 8, f1 + 8, 8):
            at = slice(OFF + b, OFF + b + 8)
            for tile in range(2):
                u = [state[tile, k, at, :] for k in range(6)]
                v = [state[tile, 6 + k, at, :] for k in range(6)]
                for k in range(6):
                    value = VISCOUS * v[k]
                    if K_STIFF[k] == 1.0:
                        value = u[k] + value
                    elif K_STIFF[k]:
                        value = K_STIFF[k] * u[k] + value
                    wp[tile, k, at, :] = value
                for n, (lead, turn, sign, _) in enumerate(ALONG):
                    wp[tile, 6 + n, at, :] = sign * u[lead] - 0.5 * u[turn]
        for b in range(f0 - 8, f1, 8):
            at = slice(OFF + b, OFF + b + 8)
            nxt = slice(OFF + b + 1, OFF + b + 9)
            prv = slice(OFF + b - 1, OFF + b + 7)

            def fluxes(base, gammas, s, pairs):
                plus, minus = list(base), list(base)
                for gamma, (lead, turn, sign, stiff) in zip(gammas, pairs):
                    plus[lead] = minus[lead] = base[lead] + (sign * stiff) * gamma
                    half = (0.5 * stiff) * gamma
                    plus[turn], minus[turn] = base[turn] + half, base[turn] - half
                out_p = [s * x for x in plus]
                out_m = [out_p[k] if plus[k] is minus[k] else s * minus[k] for k in range(6)]
                return out_p, out_m

            force = [None, None]
            for tile in range(2):
                if last_step and tile == 1:
                    continue
                u = {k: state[tile, k, at, :] for k in (1, 2, 3, 5)}
                base = [wp[tile, k, nxt, :] - wp[tile, k, at, :] for k in range(6)]
                gammas = [
                    wp[tile, 6 + n, nxt, :] - (sign * u[lead] + 0.5 * u[turn])
                    for n, (lead, turn, sign, _) in enumerate(ALONG)
                ]
                s = hd[tile, at, :] + hd[tile, nxt, :]
                plus, minus = fluxes(base, gammas, s, ALONG)
                for k in range(6):
                    fm[tile, k, at, :] = minus[k]
                if b >= f0:
                    force[tile] = [plus[k] - fm[tile, k, prv, :] for k in range(6)]
            if b < f0:
                continue
            u = [[state[tile, k, at, :] for k in range(6)] for tile in range(2)]
            w = [[wp[tile, k, at, :] for k in range(6)] for tile in range(2)]
            w_next = [after((w[0][k], w[1][k])) for k in range(6)]
            p_next = [
                after(tuple(sign * u[tile][lead] - 0.5 * u[tile][turn] for tile in range(2)))
                for lead, turn, sign, _ in ACROSS
            ]
            h = tuple(hd[tile, at, :] for tile in range(2))
            h_next = after(h)
            plus, minus = [], []
            for tile in range(2):
                base = [w_next[k][tile] - w[tile][k] for k in range(6)]
                gammas = [
                    p_next[n][tile] - (sign * u[tile][lead] + 0.5 * u[tile][turn])
                    for n, (lead, turn, sign, _) in enumerate(ACROSS)
                ]
                one_p, one_m = fluxes(base, gammas, h[tile] + h_next[tile], ACROSS)
                plus.append(one_p)
                minus.append(one_m)
            minus_prev = [before((minus[0][k], minus[1][k])) for k in range(6)]
            for tile in range(2):
                if last_step and tile == 1:
                    continue
                cols = slice(tile * LANES, (tile + 1) * LANES)
                dt = rate[b : b + 8, cols]
                total = [force[tile][k] + plus[tile][k] - minus_prev[k][tile] for k in range(6)]
                grip = 2.0 * ext[tile, 14, at, :]
                total[0] = total[0] + grip * (1.5 - u[tile][0])
                total[2] = total[2] + grip * (-0.5 - u[tile][2])
                for k in range(6):
                    v_new = KEEP * state[tile, 6 + k, at, :] + dt * total[k]
                    u_new = u[tile][k] + dt * v_new
                    if last_step:
                        out_v[k, b - PAD : b - PAD + 8, :] = v_new
                        out_u[k, b - PAD : b - PAD + 8, :] = u_new
                    else:
                        after_state[tile, 6 + k, at, :] = v_new
                        after_state[tile, k, at, :] = u_new
        state = ext2


def tables(count_x, count_y):
    pos_x = jnp.arange(ROWS) + lax.axis_index("transit") * CX - PAD
    in_x = (pos_x >= 0) & (pos_x < count_x)
    ring = jnp.arange(2 * LANES)
    pos_y = lax.axis_index("lateral") * CY + jnp.where(ring < 192, ring, ring - 2 * LANES)
    in_y = (pos_y >= 0) & (pos_y < count_y)

    def weight(offset, inside):
        dist = offset.astype(F32)
        return jnp.where((jnp.abs(offset) <= RADIUS) & inside, jnp.exp(-dist * dist / 32.0), 0.0)

    row = jnp.arange(ROWS)
    along = weight(row[None, :] - row[:, None], in_x[None, :])
    across = weight((ring[:, None] - ring[None, :] + LANES) % (2 * LANES) - LANES, in_y[:, None])
    cover = jnp.sum(along, 1)[:, None] * jnp.sum(across, 0)[None, :]
    inside = in_x[:, None] & in_y[None, :]
    cover = jnp.where(inside, cover, 1.0)
    decay = jnp.where(inside, -1.0 / (24.0 * cover), 0.0)
    rate = jnp.where(inside, DT, 0.0)

    def parts(x):
        high = lax.reduce_precision(x, 8, 7)
        return high.astype(BF16), (x - high).astype(BF16)

    bands = []
    for e0, e1, d0, d1, _, _ in STEP_ROWS:
        high, low = parts(along[d0:d1, e0:e1])
        bands.append(jnp.concatenate([jnp.concatenate([high, high], 1), jnp.concatenate([low, low], 1)], 0))
    high, low = parts(across)
    return bands + [high, low, 4.0 * cover, decay, rate]


def vmem(n):
    return [pl.BlockSpec(memory_space=pltpu.VMEM)] * n


def on_device(displacement, velocity, damage, strength, contact, flaw_cells):
    params = pltpu.CompilerParams(vmem_limit_bytes=48 * 1024 * 1024)
    shape = jax.ShapeDtypeStruct
    tile = shape((CX, CY), F32)
    send_a, send_b, *own = pl.pallas_call(
        pack_kernel,
        out_shape=[shape((SLAB, LANES), F32)] * 2
        + [shape((6, CX, CY), F32)] * 2
        + [tile, tile, shape((CX, CY), jnp.int32)],
        in_specs=[pl.BlockSpec(memory_space=pltpu.HBM)] * 6,
        out_specs=vmem(7),
        scratch_shapes=[
            pltpu.VMEM((CX, CY), F32),
            pltpu.SMEM(flaw_cells.shape, jnp.int32),
            pltpu.SemaphoreType.DMA((6,)),
        ],
        compiler_params=params,
        name="pack_rows",
    )(*(pltpu.with_memory_space_constraint(x, pltpu.HBM) for x in (flaw_cells, displacement, velocity, damage, strength, contact)))
    got = swap((send_a, send_b), "transit")
    side = pl.pallas_call(
        edge_kernel,
        out_shape=[shape((ROWS, 2 * LANES), F32)] * 2,
        in_specs=vmem(7),
        out_specs=vmem(2),
        scratch_shapes=[pltpu.VMEM((15, HELD, LANES), F32)],
        compiler_params=params,
        name="pack_columns",
    )(*own, *got)
    side = swap(side, "lateral")
    table = tables(CX * lax.axis_size("transit"), CY * lax.axis_size("lateral"))
    out = pl.pallas_call(
        step_kernel,
        out_shape=[shape((6, CX, CY), F32)] * 2 + [shape((CX, CY), F32)],
        in_specs=vmem(16),
        out_specs=vmem(3),
        scratch_shapes=[
            pltpu.VMEM((2, 15, HELD, LANES), F32),
            pltpu.VMEM((2, 12, HELD, LANES), F32),
            pltpu.VMEM((8, LANES), F32),
            pltpu.VMEM((2, 8, HELD, LANES), F32),
            pltpu.VMEM((2, 6, HELD, LANES), F32),
            pltpu.VMEM((2, HELD, LANES), F32),
            pltpu.VMEM((12, 2 * ROWS, 2 * LANES), BF16),
            pltpu.VMEM((12 * 96, 2 * LANES), BF16),
            pltpu.VMEM((12 * 96, 2 * LANES), BF16),
            pltpu.VMEM((12 * 96, 2 * LANES), F32),
        ],
        compiler_params=params,
        name="two_steps",
    )(*own, *got, *side, *table)
    return tuple(out)


def solution(mesh):
    return jax.shard_map(
        on_device,
        mesh=mesh,
        in_specs=(
            P(None, "transit", "lateral"),
            P(None, "transit", "lateral"),
            P("transit", "lateral"),
            P("transit", "lateral"),
            P("transit", "lateral"),
            P("transit", "lateral", None),
        ),
        out_specs=(
            P(None, "transit", "lateral"),
            P(None, "transit", "lateral"),
            P("transit", "lateral"),
        ),
        check_vma=False,
    )
```

```python
import functools

import jax
import jax.numpy as jnp
from jax import lax
from jax.experimental import pallas as pl
from jax.experimental.pallas import tpu as pltpu
from jax.sharding import PartitionSpec as P

RADIUS = 8
CX, CY = 64, 128
WIDE, NEAR = 20, 11
PAD = 24
ROWS = CX + 2 * PAD
OFF = 8
HELD = ROWS + 2 * OFF
LANES = 128
SLAB = 224
K_STIFF = (1.0, 1.0, 0.0, 0.5, 0.5, 0.2)
VISCOUS = 0.2
KEEP = 0.95
DT = 0.4
ALONG = ((2, 3, 1.0, 0.8), (1, 5, 1.0, 0.3))
ACROSS = ((2, 4, 1.0, 0.8), (0, 5, -1.0, 0.3))
STEP_ROWS = ((0, 112, 8, 104, 8, 104), (8, 104, 16, 96, 24, 88))
F32, BF16 = jnp.float32, jnp.bfloat16


def halo_of(field):
    return WIDE if field < 6 else NEAR


def slab_start(field):
    return WIDE * field if field < 6 else 6 * WIDE + NEAR * (field - 6)


def swap(block, axis):
    count = lax.axis_size(axis)
    out = []
    for first, part in zip((0, 1), block):
        pairs = []
        for i in range(first, count - 1, 2):
            pairs += [(i, i + 1), (i + 1, i)]
        out.append(lax.ppermute(part, axis, pairs))
    return out


def pack_kernel(
    flaw_in, disp_in, vel_in, dam_in, stren_in, con_in,
    out_a, out_b, disp, vel, dam, lim, con, stren, flaw, sems,
):
    sources = (flaw_in, disp_in, vel_in, dam_in, stren_in, con_in)
    copies = [
        pltpu.make_async_copy(src, dst, sems.at[n])
        for n, (src, dst) in enumerate(zip(sources, (flaw, disp, vel, dam, stren, con)))
    ]
    for copy in copies:
        copy.start()
    for copy in copies:
        copy.wait()
    node = lax.broadcasted_iota(jnp.int32, (CX, CY), 0) * CY + lax.broadcasted_iota(
        jnp.int32, (CX, CY), 1
    )
    mark = node == flaw[0, 0, 0]
    for j in range(1, flaw.shape[2]):
        mark = mark | (node == flaw[0, 0, j])
    lim[...] = stren[...] * jnp.where(mark, 0.4, 1.0)

    def field(k, rows):
        if k < 6:
            return disp[k, rows, :]
        if k < 12:
            return vel[k - 6, rows, :]
        if k == 12:
            return dam[rows, :]
        if k == 13:
            return lim[rows, :]
        return con[rows, :].astype(F32)

    def fill(out, top):
        for k in range(15):
            width = halo_of(k)
            rows = slice(0, width) if top else slice(CX - width, CX)
            start = slab_start(k)
            out[start : start + width, :] = field(k, rows)
        out[219:SLAB, :] = jnp.zeros((SLAB - 219, LANES), F32)

    even = lax.rem(lax.axis_index("transit"), 2) == 0

    @pl.when(even)
    def _():
        fill(out_a, False)
        fill(out_b, True)

    @pl.when(jnp.logical_not(even))
    def _():
        fill(out_a, True)
        fill(out_b, False)


def assemble(ext, disp, vel, dam, lim, con, got_a, got_b):
    even = lax.rem(lax.axis_index("transit"), 2) == 0
    for k in range(15):
        width, start = halo_of(k), slab_start(k)
        part_a = got_a[start : start + width, :]
        part_b = got_b[start : start + width, :]
        if k < 6:
            own = disp[k]
        elif k < 12:
            own = vel[k - 6]
        else:
            own = (dam, lim, con)[k - 12][...].astype(F32)
        low, high = OFF + PAD, OFF + PAD + CX
        ext[k, 0 : low - width, :] = jnp.zeros((low - width, LANES), F32)
        ext[k, low - width : low, :] = jnp.where(even, part_b, part_a)
        ext[k, low:high, :] = own
        ext[k, high : high + width, :] = jnp.where(even, part_a, part_b)
        ext[k, high + width : HELD, :] = jnp.zeros((HELD - high - width, LANES), F32)


def edge_kernel(disp, vel, dam, lim, con, got_a, got_b, out_a, out_b, ext):
    assemble(ext, disp, vel, dam, lim, con, got_a, got_b)
    lane = lax.broadcasted_iota(jnp.int32, (ROWS, LANES), 1)
    even = lax.rem(lax.axis_index("lateral"), 2) == 0
    for tile, fields in ((0, range(6)), (1, range(6, 15))):
        right = left = jnp.zeros((ROWS, LANES), F32)
        for n, k in enumerate(fields):
            width = halo_of(k)
            here = (lane >= n * width) & (lane < (n + 1) * width)
            block = ext[k, OFF : OFF + ROWS, :]
            right = jnp.where(here, pltpu.roll(block, (n * width - (CY - width)) % LANES, 1), right)
            left = jnp.where(here, pltpu.roll(block, n * width, 1) if n else block, left)
        cols = slice(tile * LANES, (tile + 1) * LANES)
        out_a[:, cols] = jnp.where(even, right, left)
        out_b[:, cols] = jnp.where(even, left, right)


def split(x):
    high = x.astype(BF16)
    return high, (x - high.astype(F32)).astype(BF16)


def step_kernel(
    disp, vel, dam, lim, con, got_a, got_b, side_b, side_a,
    along_1, along_2, across_hi, across_lo, cover, decay, rate,
    out_u, out_v, out_d,
    ext, ext2, mid, wp, fm, hd, energy, t_hi, t_lo, aver,
):
    assemble(ext.at[0], disp, vel, dam, lim, con, got_a, got_b)
    lane8 = lax.broadcasted_iota(jnp.int32, (8, LANES), 1)
    lane = lax.broadcasted_iota(jnp.int32, (ROWS, LANES), 1)
    even = lax.rem(lax.axis_index("lateral"), 2) == 0
    for tile, fields in ((0, range(6)), (1, range(6, 15))):
        cols = slice(tile * LANES, (tile + 1) * LANES)
        right = jnp.where(even, side_a[:, cols], side_b[:, cols])
        left = jnp.where(even, side_b[:, cols], side_a[:, cols])
        for n, k in enumerate(fields):
            width = halo_of(k)
            from_right = pltpu.roll(right, (-n * width) % LANES, 1) if n else right
            from_left = pltpu.roll(left, (CY - width - n * width) % LANES, 1)
            ext[1, k, 0:OFF, :] = jnp.zeros((OFF, LANES), F32)
            ext[1, k, OFF : OFF + ROWS, :] = jnp.where(lane < 64, from_right, from_left)
            ext[1, k, OFF + ROWS : HELD, :] = jnp.zeros((OFF, LANES), F32)
    for tile in range(2):
        for k in range(12):
            for low in (0, OFF + 104):
                ext2[tile, k, low : low + 16, :] = jnp.zeros((16, LANES), F32)
        for low in (0, HELD - 16):
            hd[tile, low : low + 16, :] = jnp.full((16, LANES), 0.5, F32)

    def after(pair):
        last = lax.broadcasted_iota(jnp.int32, pair[0].shape, 1) == LANES - 1
        r0, r1 = (pltpu.roll(x, LANES - 1, 1) for x in pair)
        return jnp.where(last, r1, r0), jnp.where(last, r0, r1)

    def before(pair):
        first = lax.broadcasted_iota(jnp.int32, pair[0].shape, 1) == 0
        r0, r1 = (pltpu.roll(x, 1, 1) for x in pair)
        return jnp.where(first, r1, r0), jnp.where(first, r0, r1)

    state, after_state = ext, ext2
    for step, (e0, e1, d0, d1, f0, f1) in enumerate(STEP_ROWS):
        last_step = step == 1
        span = e1 - e0
        for b in range(e0, e1, 16):
            def rows(k, shift=0):
                return tuple(state[tile, k, OFF + b + shift : OFF + b + shift + 16, :] for tile in range(2))
            here = [rows(k) for k in range(6)]
            dx = [tuple(p - m for p, m in zip(rows(k, 1), rows(k, -1))) for k in range(5)]
            dy = [tuple(p - m for p, m in zip(after(here[k]), before(here[k]))) for k in range(5)]
            for tile in range(2):
                x = [v[tile] for v in dx]
                y = [v[tile] for v in dy]
                c = [v[tile] for v in here]
                plane = (x[0], y[1], y[0] + x[1])
                bend = (x[3], y[4], y[3] + x[4])
                e7 = x[2] - 2.0 * c[3]
                e8 = y[2] - 2.0 * c[4]
                e9 = 0.5 * (x[1] - y[0]) - 2.0 * c[5]
                prods = []
                for p, q in zip(plane, bend):
                    prods += [p * p, p * q, q * q]
                prods += [e7 * e7, e8 * e8, e9 * e9]
                for ch, value in enumerate(prods):
                    high, low = split(value)
                    cols = slice(tile * LANES, (tile + 1) * LANES)
                    energy[ch, b - e0 : b - e0 + 16, cols] = high
                    energy[ch, span + b - e0 : span + b - e0 + 16, cols] = low
        band = along_2 if last_step else along_1
        n_out = d1 - d0
        for ch in range(12):
            both = jnp.dot(band[...], energy[ch, 0 : 2 * span, :], preferred_element_type=F32)
            high, low = split(both[:n_out] + both[n_out:])
            t_hi[ch * n_out : (ch + 1) * n_out, :] = high
            t_lo[ch * n_out : (ch + 1) * n_out, :] = low
        total = 12 * n_out
        aver[0:total, :] = (
            jnp.dot(t_hi[0:total, :], across_hi[...], preferred_element_type=F32)
            + jnp.dot(t_lo[0:total, :], across_hi[...], preferred_element_type=F32)
            + jnp.dot(t_hi[0:total, :], across_lo[...], preferred_element_type=F32)
        )
        for b in range(d0, d1, 8):
            for tile in range(2):
                cols = slice(tile * LANES, (tile + 1) * LANES)
                at = slice(OFF + b, OFF + b + 8)
                def mean(ch):
                    start = ch * n_out + b - d0
                    return aver[start : start + 8, cols]
                level = state[tile, 13, at, :] if step == 0 else ext[tile, 13, at, :]
                level = level * cover[b : b + 8, cols]
                driving = jnp.zeros((8, LANES), F32)
                for comp, threshold in enumerate((0.6, 0.6, 1.2)):
                    p, q, r = (mean(3 * comp + n) for n in range(3))
                    base = p - threshold * level
                    for depth in (0.75, 0.25):
                        centre = base + (depth * depth) * r
                        swing = (2.0 * depth) * q
                        driving += jnp.maximum(centre + swing, 0.0) + jnp.maximum(centre - swing, 0.0)
                    if comp == 2:
                        driving += jnp.maximum(r - level, 0.0)
                for ch, threshold in ((9, 1.5), (10, 1.5), (11, 1.2)):
                    driving += jnp.maximum(mean(ch) - threshold * level, 0.0)
                new = jnp.maximum(
                    ext[tile, 12, at, :], 1.0 - jnp.exp(driving * decay[b : b + 8, cols])
                )
                ext[tile, 12, at, :] = new
                hd[tile, at, :] = 0.5 - 0.5 * new
                if last_step and tile == 0 and PAD <= b < PAD + CX:
                    out_d[b - PAD : b - PAD + 8, :] = new
        for b in range(f0 - 8, f1 + 8, 8):
            at = slice(OFF + b, OFF + b + 8)
            for tile in range(2):
                u = [state[tile, k, at, :] for k in range(6)]
                v = [state[tile, 6 + k, at, :] for k in range(6)]
                for k in range(6):
                    value = VISCOUS * v[k]
                    if K_STIFF[k] == 1.0:
                        value = u[k] + value
                    elif K_STIFF[k]:
                        value = K_STIFF[k] * u[k] + value
                    wp[tile, k, at, :] = value
                for n, (lead, turn, sign, _) in enumerate(ALONG):
                    wp[tile, 6 + n, at, :] = sign * u[lead] - 0.5 * u[turn]
        for b in range(f0 - 8, f1, 8):
            at = slice(OFF + b, OFF + b + 8)
            nxt = slice(OFF + b + 1, OFF + b + 9)
            prv = slice(OFF + b - 1, OFF + b + 7)

            def fluxes(base, gammas, s, pairs):
                plus, minus = list(base), list(base)
                for gamma, (lead, turn, sign, stiff) in zip(gammas, pairs):
                    plus[lead] = minus[lead] = base[lead] + (sign * stiff) * gamma
                    half = (0.5 * stiff) * gamma
                    plus[turn], minus[turn] = base[turn] + half, base[turn] - half
                out_p = [s * x for x in plus]
                out_m = [out_p[k] if plus[k] is minus[k] else s * minus[k] for k in range(6)]
                return out_p, out_m

            force = [None, None]
            for tile in range(2):
                if last_step and tile == 1:
                    continue
                u = {k: state[tile, k, at, :] for k in (1, 2, 3, 5)}
                base = [wp[tile, k, nxt, :] - wp[tile, k, at, :] for k in range(6)]
                gammas = [
                    wp[tile, 6 + n, nxt, :] - (sign * u[lead] + 0.5 * u[turn])
                    for n, (lead, turn, sign, _) in enumerate(ALONG)
                ]
                s = hd[tile, at, :] + hd[tile, nxt, :]
                plus, minus = fluxes(base, gammas, s, ALONG)
                for k in range(6):
                    fm[tile, k, at, :] = minus[k]
                if b >= f0:
                    force[tile] = [plus[k] - fm[tile, k, prv, :] for k in range(6)]
            if b < f0:
                continue
            u = [[state[tile, k, at, :] for k in range(6)] for tile in range(2)]
            w = [[wp[tile, k, at, :] for k in range(6)] for tile in range(2)]
            w_next = [after((w[0][k], w[1][k])) for k in range(6)]
            p_next = [
                after(tuple(sign * u[tile][lead] - 0.5 * u[tile][turn] for tile in range(2)))
                for lead, turn, sign, _ in ACROSS
            ]
            h = tuple(hd[tile, at, :] for tile in range(2))
            h_next = after(h)
            plus, minus = [], []
            for tile in range(2):
                base = [w_next[k][tile] - w[tile][k] for k in range(6)]
                gammas = [
                    p_next[n][tile] - (sign * u[tile][lead] + 0.5 * u[tile][turn])
                    for n, (lead, turn, sign, _) in enumerate(ACROSS)
                ]
                one_p, one_m = fluxes(base, gammas, h[tile] + h_next[tile], ACROSS)
                plus.append(one_p)
                minus.append(one_m)
            minus_prev = [before((minus[0][k], minus[1][k])) for k in range(6)]
            for tile in range(2):
                if last_step and tile == 1:
                    continue
                cols = slice(tile * LANES, (tile + 1) * LANES)
                dt = rate[b : b + 8, cols]
                total = [force[tile][k] + plus[tile][k] - minus_prev[k][tile] for k in range(6)]
                grip = 2.0 * ext[tile, 14, at, :]
                total[0] = total[0] + grip * (1.5 - u[tile][0])
                total[2] = total[2] + grip * (-0.5 - u[tile][2])
                for k in range(6):
                    v_new = KEEP * state[tile, 6 + k, at, :] + dt * total[k]
                    u_new = u[tile][k] + dt * v_new
                    if last_step:
                        out_v[k, b - PAD : b - PAD + 8, :] = v_new
                        out_u[k, b - PAD : b - PAD + 8, :] = u_new
                    else:
                        after_state[tile, 6 + k, at, :] = v_new
                        after_state[tile, k, at, :] = u_new
        state = ext2


def tables(count_x, count_y):
    pos_x = jnp.arange(ROWS) + lax.axis_index("transit") * CX - PAD
    in_x = (pos_x >= 0) & (pos_x < count_x)
    ring = jnp.arange(2 * LANES)
    pos_y = lax.axis_index("lateral") * CY + jnp.where(ring < 192, ring, ring - 2 * LANES)
    in_y = (pos_y >= 0) & (pos_y < count_y)

    def weight(offset, inside):
        dist = offset.astype(F32)
        return jnp.where((jnp.abs(offset) <= RADIUS) & inside, jnp.exp(-dist * dist / 32.0), 0.0)

    row = jnp.arange(ROWS)
    along = weight(row[None, :] - row[:, None], in_x[None, :])
    across = weight((ring[:, None] - ring[None, :] + LANES) % (2 * LANES) - LANES, in_y[:, None])
    cover = jnp.sum(along, 1)[:, None] * jnp.sum(across, 0)[None, :]
    inside = in_x[:, None] & in_y[None, :]
    cover = jnp.where(inside, cover, 1.0)
    decay = jnp.where(inside, -1.0 / (24.0 * cover), 0.0)
    rate = jnp.where(inside, DT, 0.0)

    def parts(x):
        high = lax.reduce_precision(x, 8, 7)
        return high.astype(BF16), (x - high).astype(BF16)

    bands = []
    for e0, e1, d0, d1, _, _ in STEP_ROWS:
        high, low = parts(along[d0:d1, e0:e1])
        bands.append(jnp.concatenate([jnp.concatenate([high, high], 1), jnp.concatenate([low, low], 1)], 0))
    high, low = parts(across)
    return bands + [high, low, 4.0 * cover, decay, rate]


def vmem(n):
    return [pl.BlockSpec(memory_space=pltpu.VMEM)] * n


def on_device(displacement, velocity, damage, strength, contact, flaw_cells):
    params = pltpu.CompilerParams(vmem_limit_bytes=48 * 1024 * 1024)
    shape = jax.ShapeDtypeStruct
    tile = shape((CX, CY), F32)
    send_a, send_b, *own = pl.pallas_call(
        pack_kernel,
        out_shape=[shape((SLAB, LANES), F32)] * 2
        + [shape((6, CX, CY), F32)] * 2
        + [tile, tile, shape((CX, CY), jnp.int32)],
        in_specs=[pl.BlockSpec(memory_space=pltpu.HBM)] * 6,
        out_specs=vmem(7),
        scratch_shapes=[
            pltpu.VMEM((CX, CY), F32),
            pltpu.SMEM(flaw_cells.shape, jnp.int32),
            pltpu.SemaphoreType.DMA((6,)),
        ],
        compiler_params=params,
        name="pack_rows",
    )(*(pltpu.with_memory_space_constraint(x, pltpu.HBM) for x in (flaw_cells, displacement, velocity, damage, strength, contact)))
    got = swap((send_a, send_b), "transit")
    side = pl.pallas_call(
        edge_kernel,
        out_shape=[shape((ROWS, 2 * LANES), F32)] * 2,
        in_specs=vmem(7),
        out_specs=vmem(2),
        scratch_shapes=[pltpu.VMEM((15, HELD, LANES), F32)],
        compiler_params=params,
        name="pack_columns",
    )(*own, *got)
    side = swap(side, "lateral")
    table = tables(CX * lax.axis_size("transit"), CY * lax.axis_size("lateral"))
    out = pl.pallas_call(
        step_kernel,
        out_shape=[shape((6, CX, CY), F32)] * 2 + [shape((CX, CY), F32)],
        in_specs=vmem(16),
        out_specs=vmem(3),
        scratch_shapes=[
            pltpu.VMEM((2, 15, HELD, LANES), F32),
            pltpu.VMEM((2, 12, HELD, LANES), F32),
            pltpu.VMEM((8, LANES), F32),
            pltpu.VMEM((2, 8, HELD, LANES), F32),
            pltpu.VMEM((2, 6, HELD, LANES), F32),
            pltpu.VMEM((2, HELD, LANES), F32),
            pltpu.VMEM((12, 2 * ROWS, 2 * LANES), BF16),
            pltpu.VMEM((12 * 96, 2 * LANES), BF16),
            pltpu.VMEM((12 * 96, 2 * LANES), BF16),
            pltpu.VMEM((12 * 96, 2 * LANES), F32),
        ],
        compiler_params=params,
        name="two_steps",
    )(*own, *got, *side[::-1], *table)
    return tuple(out)


def solution(mesh):
    return jax.shard_map(
        on_device,
        mesh=mesh,
        in_specs=(
            P(None, "transit", "lateral"),
            P(None, "transit", "lateral"),
            P("transit", "lateral"),
            P("transit", "lateral"),
            P("transit", "lateral"),
            P("transit", "lateral", None),
        ),
        out_specs=(
            P(None, "transit", "lateral"),
            P(None, "transit", "lateral"),
            P("transit", "lateral"),
        ),
        check_vma=False,
    )
```

```python
import functools

import jax
import jax.numpy as jnp
from jax import lax
from jax.experimental import pallas as pl
from jax.experimental.pallas import tpu as pltpu
from jax.sharding import PartitionSpec as P

RADIUS = 8
CX, CY = 64, 128
WIDE, NEAR = 20, 11
PAD = 24
EDGE = 32
SPAN = CY + 2 * EDGE
OFF = EDGE + 8
HELD = CY + 2 * OFF
LANES = 128
SLAB = 224
K_STIFF = (1.0, 1.0, 0.0, 0.5, 0.5, 0.2)
VISCOUS = 0.2
KEEP = 0.95
DT = 0.4
ALONG = ((2, 3, 1.0, 0.8), (1, 5, 1.0, 0.3))
ACROSS = ((2, 4, 1.0, 0.8), (0, 5, -1.0, 0.3))
F32, BF16 = jnp.float32, jnp.bfloat16


def halo_of(field):
    return WIDE if field < 6 else NEAR


def slab_start(field):
    return WIDE * field if field < 6 else 6 * WIDE + NEAR * (field - 6)


def swap(block, axis):
    count = lax.axis_size(axis)
    out = []
    for first, part in zip((0, 1), block):
        pairs = []
        for i in range(first, count - 1, 2):
            pairs += [(i, i + 1), (i + 1, i)]
        out.append(lax.ppermute(part, axis, pairs))
    return out


def pack_kernel(
    flaw_in, disp_in, vel_in, dam_in, stren_in, con_in,
    out_a, out_b, disp, vel, dam, lim, con, stren, flaw, sems,
):
    sources = (flaw_in, disp_in, vel_in, dam_in, stren_in, con_in)
    copies = [
        pltpu.make_async_copy(src, dst, sems.at[n])
        for n, (src, dst) in enumerate(zip(sources, (flaw, disp, vel, dam, stren, con)))
    ]
    for copy in copies:
        copy.start()
    for copy in copies:
        copy.wait()
    node = lax.broadcasted_iota(jnp.int32, (CX, CY), 0) * CY + lax.broadcasted_iota(
        jnp.int32, (CX, CY), 1
    )
    mark = node == flaw[0, 0, 0]
    for j in range(1, flaw.shape[2]):
        mark = mark | (node == flaw[0, 0, j])
    lim[...] = stren[...] * jnp.where(mark, 0.4, 1.0)

    def field(k, rows):
        if k < 6:
            return disp[k, rows, :]
        if k < 12:
            return vel[k - 6, rows, :]
        if k == 12:
            return dam[rows, :]
        if k == 13:
            return lim[rows, :]
        return con[rows, :].astype(F32)

    def fill(out, top):
        for k in range(15):
            width = halo_of(k)
            rows = slice(0, width) if top else slice(CX - width, CX)
            start = slab_start(k)
            out[start : start + width, :] = field(k, rows)
        out[219:SLAB, :] = jnp.zeros((SLAB - 219, LANES), F32)

    even = lax.rem(lax.axis_index("transit"), 2) == 0

    @pl.when(even)
    def _():
        fill(out_a, False)
        fill(out_b, True)

    @pl.when(jnp.logical_not(even))
    def _():
        fill(out_a, True)
        fill(out_b, False)


def edge_kernel(disp, vel, dam, lim, con, got_a, got_b, out_a, out_b, flat, ext):
    even = lax.rem(lax.axis_index("transit"), 2) == 0
    even_l = lax.rem(lax.axis_index("lateral"), 2) == 0
    for k in range(15):
        width, start = halo_of(k), slab_start(k)
        part_a = got_a[start : start + width, :]
        part_b = got_b[start : start + width, :]
        if k < 6:
            own = disp[k]
        elif k < 12:
            own = vel[k - 6]
        else:
            own = (dam, lim, con)[k - 12][...].astype(F32)
        low, high = PAD, PAD + CX
        ext[k, 0 : low - width, :] = jnp.zeros((low - width, LANES), F32)
        ext[k, low - width : low, :] = jnp.where(even, part_b, part_a)
        ext[k, low:high, :] = own
        ext[k, high : high + width, :] = jnp.where(even, part_a, part_b)
        ext[k, high + width : LANES, :] = jnp.zeros((LANES - high - width, LANES), F32)
        turned = ext[k].T
        flat[k, 8 : 8 + CY, :] = turned
        flat[k, 0:8, :] = jnp.zeros((8, LANES), F32)
        flat[k, 8 + CY : 16 + CY, :] = jnp.zeros((8, LANES), F32)
        right, left = turned[CY - width :, :], turned[:width, :]
        out_a[start : start + width, :] = jnp.where(even_l, right, left)
        out_b[start : start + width, :] = jnp.where(even_l, left, right)
    for out in (out_a, out_b):
        out[219:SLAB, :] = jnp.zeros((SLAB - 219, LANES), F32)


def split(x):
    high = x.astype(BF16)
    return high, (x - high.astype(F32)).astype(BF16)


def next_lane(x):
    return pltpu.roll(x, LANES - 1, 1)


def prev_lane(x):
    return pltpu.roll(x, 1, 1)


def products(get, put):
    c = [get(k, 0) for k in range(6)]
    x = [next_lane(c[k]) - prev_lane(c[k]) for k in range(5)]
    y = [get(k, 1) - get(k, -1) for k in range(5)]
    plane = (x[0], y[1], y[0] + x[1])
    bend = (x[3], y[4], y[3] + x[4])
    e7 = x[2] - 2.0 * c[3]
    e8 = y[2] - 2.0 * c[4]
    e9 = 0.5 * (x[1] - y[0]) - 2.0 * c[5]
    values = []
    for p, q in zip(plane, bend):
        values += [p * p, p * q, q * q]
    for ch, value in enumerate(values + [e7 * e7, e8 * e8, e9 * e9]):
        high, low = split(value)
        put(ch, slice(0, LANES), high)
        put(ch, slice(LANES, 2 * LANES), low)


def lane_sums(energy, turned, rows, band):
    for ch in range(12):
        both = jnp.dot(energy[ch, 0:rows, :], band[...], preferred_element_type=F32)
        high, low = split(both[:, :LANES] + both[:, LANES:])
        cols = slice(ch % 2 * LANES, (ch % 2 + 1) * LANES)
        turned[ch // 2, 0:rows, cols] = high
        turned[ch // 2, rows : 2 * rows, cols] = low


def row_sums(turned, pair, rows, first, second):
    return jnp.dot(first[...], turned[pair, 0 : 2 * rows, :], preferred_element_type=F32) + jnp.dot(
        second[...], turned[pair, 0:rows, :], preferred_element_type=F32
    )


def inner_kernel(flat, band, first, second, partial, energy, turned):
    for b in range(0, CY, 16):
        def get(k, shift):
            return flat[k, 8 + b + shift : 24 + b + shift, :]

        def put(ch, cols, value):
            energy[ch, b : b + 16, cols] = value

        products(get, put)
    lane_sums(energy, turned, CY, band)
    for pair in range(6):
        partial[pair] = row_sums(turned, pair, CY, first, second)


def step_kernel(
    flat, partial, side_b, side_a, band, rim_1, rim_2, all_1, all_2, cover, decay, rate,
    out_u, out_v, out_d,
    ext, ext2, wp, fm, hd, energy, turned, aver, final,
):
    even = lax.rem(lax.axis_index("lateral"), 2) == 0
    for k in range(15):
        width, start = halo_of(k), slab_start(k)
        part_a = side_a[start : start + width, :]
        part_b = side_b[start : start + width, :]
        ext[k, 0 : OFF - width, :] = jnp.zeros((OFF - width, LANES), F32)
        ext[k, OFF - width : OFF, :] = jnp.where(even, part_b, part_a)
        ext[k, OFF : OFF + CY, :] = flat[k, 8 : 8 + CY, :]
        ext[k, OFF + CY : OFF + CY + width, :] = jnp.where(even, part_a, part_b)
        ext[k, OFF + CY + width : HELD, :] = jnp.zeros((OFF - width, LANES), F32)
    for low in (-24, 144):
        for k in range(12):
            ext2[k, OFF + low : OFF + low + 8, :] = jnp.zeros((8, LANES), F32)
        hd[OFF + low : OFF + low + 8, :] = jnp.full((8, LANES), 0.5, F32)

    state = ext
    for last_step in (False, True):
        if last_step:
            starts, n_in, d0, d1, f0, f1 = range(-16, 144, 16), 160, -8, 136, 0, CY
        else:
            starts, n_in, d0, d1, f0, f1 = (-32, -16, 0, 112, 128, 144), 96, -16, 144, -16, 144
        for n, b in enumerate(starts):
            def get(k, shift):
                return state[k, OFF + b + shift : OFF + b + shift + 16, :]

            def put(ch, cols, value):
                energy[ch, 16 * n : 16 * n + 16, cols] = value

            products(get, put)
        lane_sums(energy, turned, n_in, band)
        n_out = d1 - d0
        for pair in range(6):
            if last_step:
                aver[pair, 0:n_out, :] = row_sums(turned, pair, n_in, all_1, all_2)
            else:
                aver[pair, 0:n_out, :] = partial[pair] + row_sums(turned, pair, n_in, rim_1, rim_2)
        for b in range(d0, d1, 8):
            at = slice(OFF + b, OFF + b + 8)
            tab = slice(EDGE + b, EDGE + b + 8)

            def mean(ch):
                cols = slice(ch % 2 * LANES, (ch % 2 + 1) * LANES)
                return aver[ch // 2, b - d0 : b - d0 + 8, cols]

            level = ext[13, at, :] * cover[tab, :]
            driving = jnp.zeros((8, LANES), F32)
            for comp, threshold in enumerate((0.6, 0.6, 1.2)):
                p, q, r = (mean(3 * comp + n) for n in range(3))
                base = p - threshold * level
                for depth in (0.75, 0.25):
                    centre = base + (depth * depth) * r
                    swing = (2.0 * depth) * q
                    driving += jnp.maximum(centre + swing, 0.0) + jnp.maximum(centre - swing, 0.0)
                if comp == 2:
                    driving += jnp.maximum(r - level, 0.0)
            for ch, threshold in ((9, 1.5), (10, 1.5), (11, 1.2)):
                driving += jnp.maximum(mean(ch) - threshold * level, 0.0)
            new = jnp.maximum(ext[12, at, :], 1.0 - jnp.exp(driving * decay[tab, :]))
            ext[12, at, :] = new
            hd[at, :] = 0.5 - 0.5 * new
        for b in range(f0 - 8, f1 + 8, 8):
            at = slice(OFF + b, OFF + b + 8)
            u = [state[k, at, :] for k in range(6)]
            for k in range(6):
                value = VISCOUS * state[6 + k, at, :]
                if K_STIFF[k] == 1.0:
                    value = u[k] + value
                elif K_STIFF[k]:
                    value = K_STIFF[k] * u[k] + value
                wp[k, at, :] = value
            for n, (lead, turn, sign, _) in enumerate(ACROSS):
                wp[6 + n, at, :] = sign * u[lead] - 0.5 * u[turn]
        for b in range(f0 - 8, f1, 8):
            at = slice(OFF + b, OFF + b + 8)
            nxt = slice(OFF + b + 1, OFF + b + 9)
            prv = slice(OFF + b - 1, OFF + b + 7)

            def fluxes(base, gammas, s, pairs):
                plus, minus = list(base), list(base)
                for gamma, (lead, turn, sign, stiff) in zip(gammas, pairs):
                    plus[lead] = minus[lead] = base[lead] + (sign * stiff) * gamma
                    half = (0.5 * stiff) * gamma
                    plus[turn], minus[turn] = base[turn] + half, base[turn] - half
                out_p = [s * x for x in plus]
                return out_p, [out_p[k] if plus[k] is minus[k] else s * minus[k] for k in range(6)]

            u = [state[k, at, :] for k in range(6)]
            w = [wp[k, at, :] for k in range(6)]
            h = hd[at, :]
            base = [wp[k, nxt, :] - w[k] for k in range(6)]
            gammas = [
                wp[6 + n, nxt, :] - (sign * u[lead] + 0.5 * u[turn])
                for n, (lead, turn, sign, _) in enumerate(ACROSS)
            ]
            plus, minus = fluxes(base, gammas, h + hd[nxt, :], ACROSS)
            for k in range(6):
                fm[k, at, :] = minus[k]
            if b < f0:
                continue
            total = [plus[k] - fm[k, prv, :] for k in range(6)]
            base = [next_lane(w[k]) - w[k] for k in range(6)]
            gammas = [
                next_lane(sign * u[lead] - 0.5 * u[turn]) - (sign * u[lead] + 0.5 * u[turn])
                for lead, turn, sign, _ in ALONG
            ]
            plus, minus = fluxes(base, gammas, h + next_lane(h), ALONG)
            total = [total[k] + plus[k] - prev_lane(minus[k]) for k in range(6)]
            dt = rate[EDGE + b : EDGE + b + 8, :]
            grip = 2.0 * ext[14, at, :]
            total[0] = total[0] + grip * (1.5 - u[0])
            total[2] = total[2] + grip * (-0.5 - u[2])
            for k in range(6):
                v_new = KEEP * state[6 + k, at, :] + dt * total[k]
                u_new = u[k] + dt * v_new
                if last_step:
                    final[6 + k, b : b + 8, :] = v_new
                    final[k, b : b + 8, :] = u_new
                else:
                    ext2[6 + k, at, :] = v_new
                    ext2[k, at, :] = u_new
        state = ext2
    for k in range(6):
        out_u[k] = final[k].T[PAD : PAD + CX, :]
        out_v[k] = final[6 + k].T[PAD : PAD + CX, :]
    out_d[...] = ext[12, OFF : OFF + CY, :].T[PAD : PAD + CX, :]


def tables(count_x, count_y):
    lane, row = jnp.arange(LANES), jnp.arange(SPAN)
    pos_x = lane + lax.axis_index("transit") * CX - PAD
    pos_y = row + lax.axis_index("lateral") * CY - EDGE
    in_x = (pos_x >= 0) & (pos_x < count_x)
    in_y = (pos_y >= 0) & (pos_y < count_y)

    def weight(offset, inside):
        dist = offset.astype(F32)
        return jnp.where((jnp.abs(offset) <= RADIUS) & inside, jnp.exp(-dist * dist / 32.0), 0.0)

    def parts(x):
        high = lax.reduce_precision(x, 8, 7)
        return high.astype(BF16), (x - high).astype(BF16)

    def beside(x, y):
        return jnp.concatenate([x, y], 1)

    along = weight(lane[:, None] - lane[None, :], in_x[:, None])
    across = weight(row[None, :] - row[:, None], in_y[None, :])
    cover = jnp.sum(across, 1)[:, None] * jnp.sum(along, 0)[None, :]
    inside = in_y[:, None] & in_x[None, :]
    cover = jnp.where(inside, cover, 1.0)
    decay = jnp.where(inside, -1.0 / (24.0 * cover), 0.0)
    rate = jnp.where(inside, DT, 0.0)
    high, low = parts(along)
    band = beside(high, low)
    band = jnp.concatenate([band, band], 0)
    own = (row > EDGE) & (row < EDGE + CY - 1)
    high, low = parts(jnp.where(own[None, :], across, 0.0)[16:176, EDGE : EDGE + CY])
    own_1, own_2 = beside(high, high), low
    outer = jnp.where(own[None, :], 0.0, across)[16:176]
    high, low = parts(beside(outer[:, 0:48], outer[:, 144:192]))
    rim_1, rim_2 = beside(high, high), low
    high, low = parts(across[24:168, 16:176])
    all_1, all_2 = beside(high, high), low
    return band, (own_1, own_2), (rim_1, rim_2, all_1, all_2, 4.0 * cover, decay, rate)


def vmem(n):
    return [pl.BlockSpec(memory_space=pltpu.VMEM)] * n


def on_device(displacement, velocity, damage, strength, contact, flaw_cells):
    params = pltpu.CompilerParams(vmem_limit_bytes=48 * 1024 * 1024)
    shape = jax.ShapeDtypeStruct
    tile = shape((CX, CY), F32)
    send_a, send_b, *own = pl.pallas_call(
        pack_kernel,
        out_shape=[shape((SLAB, LANES), F32)] * 2
        + [shape((6, CX, CY), F32)] * 2
        + [tile, tile, shape((CX, CY), jnp.int32)],
        in_specs=[pl.BlockSpec(memory_space=pltpu.HBM)] * 6,
        out_specs=vmem(7),
        scratch_shapes=[
            pltpu.VMEM((CX, CY), F32),
            pltpu.SMEM(flaw_cells.shape, jnp.int32),
            pltpu.SemaphoreType.DMA((6,)),
        ],
        compiler_params=params,
        name="pack_rows",
    )(*(pltpu.with_memory_space_constraint(x, pltpu.HBM) for x in (flaw_cells, displacement, velocity, damage, strength, contact)))
    got = swap((send_a, send_b), "transit")
    side_a, side_b, flat = pl.pallas_call(
        edge_kernel,
        out_shape=[shape((SLAB, LANES), F32)] * 2 + [shape((15, 16 + CY, LANES), F32)],
        in_specs=vmem(7),
        out_specs=vmem(3),
        scratch_shapes=[pltpu.VMEM((15, LANES, LANES), F32)],
        compiler_params=params,
        name="turn_and_cut",
    )(*own, *got)
    side = swap((side_a, side_b), "lateral")
    band, of_own, table = tables(CX * lax.axis_size("transit"), CY * lax.axis_size("lateral"))
    partial = pl.pallas_call(
        inner_kernel,
        out_shape=shape((6, 160, 2 * LANES), F32),
        in_specs=vmem(4),
        out_specs=vmem(1)[0],
        scratch_shapes=[
            pltpu.VMEM((12, CY, 2 * LANES), BF16),
            pltpu.VMEM((6, 2 * CY, 2 * LANES), BF16),
        ],
        compiler_params=params,
        cost_estimate=pl.CostEstimate(flops=800_000_000, bytes_accessed=2_000_000, transcendentals=0),
        name="own_rows",
    )(flat, band, *of_own)
    out = pl.pallas_call(
        step_kernel,
        out_shape=[shape((6, CX, CY), F32)] * 2 + [shape((CX, CY), F32)],
        in_specs=vmem(12),
        out_specs=vmem(3),
        scratch_shapes=[
            pltpu.VMEM((15, HELD, LANES), F32),
            pltpu.VMEM((12, HELD, LANES), F32),
            pltpu.VMEM((8, HELD, LANES), F32),
            pltpu.VMEM((6, HELD, LANES), F32),
            pltpu.VMEM((HELD, LANES), F32),
            pltpu.VMEM((12, 160, 2 * LANES), BF16),
            pltpu.VMEM((6, 320, 2 * LANES), BF16),
            pltpu.VMEM((6, 160, 2 * LANES), F32),
            pltpu.VMEM((12, CY, LANES), F32),
        ],
        compiler_params=params,
        name="two_steps",
    )(flat, partial, *side[::-1], band, *table)
    return tuple(out)


def solution(mesh):
    return jax.shard_map(
        on_device,
        mesh=mesh,
        in_specs=(
            P(None, "transit", "lateral"),
            P(None, "transit", "lateral"),
            P("transit", "lateral"),
            P("transit", "lateral"),
            P("transit", "lateral"),
            P("transit", "lateral", None),
        ),
        out_specs=(
            P(None, "transit", "lateral"),
            P(None, "transit", "lateral"),
            P("transit", "lateral"),
        ),
        check_vma=False,
    )
```

```python
import functools

import jax
import jax.numpy as jnp
from jax import lax
from jax.experimental import pallas as pl
from jax.experimental.pallas import tpu as pltpu
from jax.sharding import PartitionSpec as P

RADIUS = 8
CX, CY = 64, 128
WIDE, NEAR = 20, 11
PAD = 24
EDGE = 32
SPAN = CY + 2 * EDGE
OFF = EDGE + 8
HELD = CY + 2 * OFF
LANES = 128
SLAB = 224
K_STIFF = (1.0, 1.0, 0.0, 0.5, 0.5, 0.2)
VISCOUS = 0.2
KEEP = 0.95
DT = 0.4
ALONG = ((2, 3, 1.0, 0.8), (1, 5, 1.0, 0.3))
ACROSS = ((2, 4, 1.0, 0.8), (0, 5, -1.0, 0.3))
F32, BF16 = jnp.float32, jnp.bfloat16


def halo_of(field):
    return WIDE if field < 6 else NEAR


def slab_start(field):
    return WIDE * field if field < 6 else 6 * WIDE + NEAR * (field - 6)


def swap(block, axis):
    count = lax.axis_size(axis)
    out = []
    for first, part in zip((0, 1), block):
        pairs = []
        for i in range(first, count - 1, 2):
            pairs += [(i, i + 1), (i + 1, i)]
        out.append(lax.ppermute(part, axis, pairs))
    return out


def weakness(rows, flaw, first_row):
    node = lax.broadcasted_iota(jnp.int32, (rows, CY), 0) * CY + lax.broadcasted_iota(
        jnp.int32, (rows, CY), 1
    )
    mark = node == flaw[0, 0, 0] - first_row * CY
    for j in range(1, flaw.shape[2]):
        mark = mark | (node == flaw[0, 0, j] - first_row * CY)
    return jnp.where(mark, 0.4, 1.0)


def run_copies(pairs, sems):
    copies = [pltpu.make_async_copy(src, dst, sems.at[n]) for n, (src, dst) in enumerate(pairs)]
    for copy in copies:
        copy.start()
    copies[0].wait()
    return copies[1:]


def pack_kernel(flaw_in, disp_in, vel_in, dam_in, stren_in, con_in, out_a, out_b, disp, vel, dam, stren, con, flaw, sems):
    pairs = [(flaw_in, flaw)]
    for side in range(2):
        wide = pl.ds(side * (CX - 24), 24)
        near = pl.ds(side * (CX - 16), 16)
        pairs.append((disp_in.at[:, wide, :], disp.at[side]))
        pairs.append((vel_in.at[:, near, :], vel.at[side]))
        for src, dst in ((dam_in, dam), (stren_in, stren), (con_in, con)):
            pairs.append((src.at[near, :], dst.at[side]))
    others = run_copies(pairs, sems)
    factors = [weakness(16, flaw, side * (CX - 16)) for side in range(2)]
    for copy in others:
        copy.wait()
    limits = [stren[side] * factors[side] for side in range(2)]

    def fill(out, side):
        for k in range(15):
            width, start = halo_of(k), slab_start(k)
            held = 24 if k < 6 else 16
            rows = slice(held - width, held) if side else slice(0, width)
            if k < 6:
                part = disp[side, k, rows, :]
            elif k < 12:
                part = vel[side, k - 6, rows, :]
            elif k == 12:
                part = dam[side, rows, :]
            elif k == 13:
                part = limits[side][rows, :]
            else:
                part = con[side, rows, :].astype(F32)
            out[start : start + width, :] = part
        out[219:SLAB, :] = jnp.zeros((SLAB - 219, LANES), F32)

    even = lax.rem(lax.axis_index("transit"), 2) == 0

    @pl.when(even)
    def _():
        fill(out_a, 1)
        fill(out_b, 0)

    @pl.when(jnp.logical_not(even))
    def _():
        fill(out_a, 0)
        fill(out_b, 1)


def load_kernel(flaw_in, disp_in, vel_in, dam_in, stren_in, con_in, disp, vel, dam, lim, con, stren, flaw, sems):
    others = run_copies(
        zip(
            (flaw_in, disp_in, vel_in, dam_in, stren_in, con_in),
            (flaw, disp, vel, dam, stren, con),
        ),
        sems,
    )
    factor = weakness(CX, flaw, 0)
    for copy in others:
        copy.wait()
    lim[...] = stren[...] * factor


def edge_kernel(disp, vel, dam, lim, con, got_a, got_b, out_a, out_b, flat, ext):
    even = lax.rem(lax.axis_index("transit"), 2) == 0
    even_l = lax.rem(lax.axis_index("lateral"), 2) == 0
    for k in range(15):
        width, start = halo_of(k), slab_start(k)
        part_a = got_a[start : start + width, :]
        part_b = got_b[start : start + width, :]
        if k < 6:
            own = disp[k]
        elif k < 12:
            own = vel[k - 6]
        else:
            own = (dam, lim, con)[k - 12][...].astype(F32)
        low, high = PAD, PAD + CX
        ext[k, 0 : low - width, :] = jnp.zeros((low - width, LANES), F32)
        ext[k, low - width : low, :] = jnp.where(even, part_b, part_a)
        ext[k, low:high, :] = own
        ext[k, high : high + width, :] = jnp.where(even, part_a, part_b)
        ext[k, high + width : LANES, :] = jnp.zeros((LANES - high - width, LANES), F32)
        turned = ext[k].T
        flat[k, 8 : 8 + CY, :] = turned
        flat[k, 0:8, :] = jnp.zeros((8, LANES), F32)
        flat[k, 8 + CY : 16 + CY, :] = jnp.zeros((8, LANES), F32)
        right, left = turned[CY - width :, :], turned[:width, :]
        out_a[start : start + width, :] = jnp.where(even_l, right, left)
        out_b[start : start + width, :] = jnp.where(even_l, left, right)
    for out in (out_a, out_b):
        out[219:SLAB, :] = jnp.zeros((SLAB - 219, LANES), F32)


def split(x):
    high = x.astype(BF16)
    return high, (x - high.astype(F32)).astype(BF16)


def next_lane(x):
    return pltpu.roll(x, LANES - 1, 1)


def prev_lane(x):
    return pltpu.roll(x, 1, 1)


def products(get, put):
    c = [get(k, 0) for k in range(6)]
    x = [next_lane(c[k]) - prev_lane(c[k]) for k in range(5)]
    y = [get(k, 1) - get(k, -1) for k in range(5)]
    plane = (x[0], y[1], y[0] + x[1])
    bend = (x[3], y[4], y[3] + x[4])
    e7 = x[2] - 2.0 * c[3]
    e8 = y[2] - 2.0 * c[4]
    e9 = 0.5 * (x[1] - y[0]) - 2.0 * c[5]
    values = []
    for p, q in zip(plane, bend):
        values += [p * p, p * q, q * q]
    for ch, value in enumerate(values + [e7 * e7, e8 * e8, e9 * e9]):
        high, low = split(value)
        put(ch, slice(0, LANES), high)
        put(ch, slice(LANES, 2 * LANES), low)


def lane_sums(energy, turned, rows, band):
    for ch in range(12):
        both = jnp.dot(energy[ch, 0:rows, :], band[...], preferred_element_type=F32)
        high, low = split(both[:, :LANES] + both[:, LANES:])
        cols = slice(ch % 2 * LANES, (ch % 2 + 1) * LANES)
        turned[ch // 2, 0:rows, cols] = high
        turned[ch // 2, rows : 2 * rows, cols] = low


def row_sums(turned, pair, rows, first, second):
    return jnp.dot(first[...], turned[pair, 0 : 2 * rows, :], preferred_element_type=F32) + jnp.dot(
        second[...], turned[pair, 0:rows, :], preferred_element_type=F32
    )


def new_damage(mean, level, old, decay):
    driving = jnp.zeros((8, LANES), F32)
    for comp, threshold in enumerate((0.6, 0.6, 1.2)):
        p, q, r = (mean(3 * comp + n) for n in range(3))
        base = p - threshold * level
        for depth in (0.75, 0.25):
            centre = base + (depth * depth) * r
            swing = (2.0 * depth) * q
            driving += jnp.maximum(centre + swing, 0.0) + jnp.maximum(centre - swing, 0.0)
        if comp == 2:
            driving += jnp.maximum(r - level, 0.0)
    for ch, threshold in ((9, 1.5), (10, 1.5), (11, 1.2)):
        driving += jnp.maximum(mean(ch) - threshold * level, 0.0)
    return jnp.maximum(old, 1.0 - jnp.exp(driving * decay))


def fluxes(base, gammas, s, pairs):
    plus, minus = list(base), list(base)
    for gamma, (lead, turn, sign, stiff) in zip(gammas, pairs):
        plus[lead] = minus[lead] = base[lead] + (sign * stiff) * gamma
        half = (0.5 * stiff) * gamma
        plus[turn], minus[turn] = base[turn] + half, base[turn] - half
    out_p = [s * x for x in plus]
    return out_p, [out_p[k] if plus[k] is minus[k] else s * minus[k] for k in range(6)]


def move(f0, f1, state, off, hd, contact, rate, wp, fm, put):
    for b in range(f0 - 8, f1 + 8, 8):
        at = slice(OFF + b, OFF + b + 8)
        here = slice(off + b, off + b + 8)
        u = [state[k, here, :] for k in range(6)]
        for k in range(6):
            value = VISCOUS * state[6 + k, here, :]
            if K_STIFF[k] == 1.0:
                value = u[k] + value
            elif K_STIFF[k]:
                value = K_STIFF[k] * u[k] + value
            wp[k, at, :] = value
        for n, (lead, turn, sign, _) in enumerate(ACROSS):
            wp[6 + n, at, :] = sign * u[lead] - 0.5 * u[turn]
    for b in range(f0 - 8, f1, 8):
        at = slice(OFF + b, OFF + b + 8)
        nxt = slice(OFF + b + 1, OFF + b + 9)
        prv = slice(OFF + b - 1, OFF + b + 7)
        here = slice(off + b, off + b + 8)
        u = [state[k, here, :] for k in range(6)]
        w = [wp[k, at, :] for k in range(6)]
        h = hd[at, :]
        base = [wp[k, nxt, :] - w[k] for k in range(6)]
        gammas = [
            wp[6 + n, nxt, :] - (sign * u[lead] + 0.5 * u[turn])
            for n, (lead, turn, sign, _) in enumerate(ACROSS)
        ]
        plus, minus = fluxes(base, gammas, h + hd[nxt, :], ACROSS)
        for k in range(6):
            fm[k, at, :] = minus[k]
        if b < f0:
            continue
        total = [plus[k] - fm[k, prv, :] for k in range(6)]
        base = [next_lane(w[k]) - w[k] for k in range(6)]
        gammas = [
            next_lane(sign * u[lead] - 0.5 * u[turn]) - (sign * u[lead] + 0.5 * u[turn])
            for lead, turn, sign, _ in ALONG
        ]
        plus, minus = fluxes(base, gammas, h + next_lane(h), ALONG)
        total = [total[k] + plus[k] - prev_lane(minus[k]) for k in range(6)]
        dt = rate[EDGE + b : EDGE + b + 8, :]
        grip = 2.0 * contact(b)
        total[0] = total[0] + grip * (1.5 - u[0])
        total[2] = total[2] + grip * (-0.5 - u[2])
        for k in range(6):
            v_new = KEEP * state[6 + k, here, :] + dt * total[k]
            put(6 + k, b, v_new)
            put(k, b, u[k] + dt * v_new)


def rows_of(ref, off, b):
    return ref[off + b : off + b + 8, :]


def harm(b, row, aver, limit, old, hd, cover, decay):
    def mean(ch):
        return aver[ch // 2, row : row + 8, ch % 2 * LANES : (ch % 2 + 1) * LANES]

    tab = slice(EDGE + b, EDGE + b + 8)
    new = new_damage(mean, limit * cover[tab, :], old, decay[tab, :])
    hd[OFF + b : OFF + b + 8, :] = 0.5 - 0.5 * new
    return new


def gather(state, off, starts, energy, turned, band):
    for n, b in enumerate(starts):
        def get(k, shift):
            return state[k, off + b + shift : off + b + shift + 16, :]

        def put(ch, cols, value):
            energy[ch, 16 * n : 16 * n + 16, cols] = value

        products(get, put)
    lane_sums(energy, turned, 16 * len(starts), band)


def inner_kernel(
    flat, band, first, second, mid_1, mid_2, cover, decay, rate,
    partial, moved, harmed_1, final, harmed_2,
    next_state, energy, turned, aver, old, wp, fm, hd,
):
    for low in (0, 120):
        hd[OFF + low : OFF + low + 8, :] = jnp.full((8, LANES), 0.5, F32)
        for k in range(6):
            next_state[k, OFF + low : OFF + low + 8, :] = jnp.zeros((8, LANES), F32)
    gather(flat, 8, range(0, CY, 16), energy, turned, band)
    for pair in range(6):
        sums = row_sums(turned, pair, CY, first, second)
        partial[pair, 0:32, :] = sums[0:32]
        aver[pair] = sums[24:136]
        partial[pair, 32:64, :] = sums[128:160]

    def contact(b):
        return rows_of(flat.at[14], 8, b)

    for b in range(8, 120, 8):
        new = harm(b, b - 8, aver, rows_of(flat.at[13], 8, b), rows_of(flat.at[12], 8, b), hd, cover, decay)
        old[b - 8 : b, :] = new
    harmed_1[0:16, :] = old[8:24, :]
    harmed_1[16:32, :] = old[88:104, :]

    def put_next(k, b, value):
        next_state[k, OFF + b : OFF + b + 8, :] = value

    move(8, 120, flat, 8, hd, contact, rate, wp, fm, put_next)
    for k in range(12):
        moved[k, 0:24, :] = next_state[k, OFF + 16 : OFF + 40, :]
        moved[k, 24:48, :] = next_state[k, OFF + 88 : OFF + 112, :]
    gather(next_state, OFF, range(8, 120, 16), energy, turned, band)
    for pair in range(6):
        aver[pair, 0:96, :] = row_sums(turned, pair, 112, mid_1, mid_2)
    for b in range(16, 112, 8):
        new = harm(b, b - 16, aver, rows_of(flat.at[13], 8, b), old[b - 8 : b, :], hd, cover, decay)
        if 24 <= b < 104:
            harmed_2[b - 24 : b - 16, :] = new

    def put_last(k, b, value):
        final[k, b - 24 : b - 16, :] = value

    move(24, 104, next_state, OFF, hd, contact, rate, wp, fm, put_last)


def step_kernel(
    flat, partial, moved, harmed_1, inner, harmed_2, side_b, side_a,
    band, rim_1, rim_2, all_1, all_2, cover, decay, rate,
    out_u, out_v, out_d,
    ext, ext2, wp, fm, hd, energy, turned, aver, final, done, sems,
):
    even = lax.rem(lax.axis_index("lateral"), 2) == 0
    for k in range(15):
        width, start = halo_of(k), slab_start(k)
        part_a = side_a[start : start + width, :]
        part_b = side_b[start : start + width, :]
        ext[k, OFF - EDGE : OFF - width, :] = jnp.zeros((EDGE - width, LANES), F32)
        ext[k, OFF - width : OFF, :] = jnp.where(even, part_b, part_a)
        for low, high in ((0, 24), (104, CY)):
            ext[k, OFF + low : OFF + high, :] = flat[k, 8 + low : 8 + high, :]
        ext[k, OFF + CY : OFF + CY + width, :] = jnp.where(even, part_a, part_b)
        ext[k, OFF + CY + width : OFF + CY + EDGE, :] = jnp.zeros((EDGE - width, LANES), F32)
    for low in (-24, 144):
        for k in range(6):
            ext2[k, OFF + low : OFF + low + 8, :] = jnp.zeros((8, LANES), F32)
        hd[OFF + low : OFF + low + 8, :] = jnp.full((8, LANES), 0.5, F32)
    for k in range(12):
        ext2[k, OFF + 16 : OFF + 40, :] = moved[k, 0:24, :]
        ext2[k, OFF + 88 : OFF + 112, :] = moved[k, 24:48, :]
        final[k, 24:104, :] = inner[k]
    for n, low in ((0, 16), (16, 96)):
        ext[12, OFF + low : OFF + low + 16, :] = harmed_1[n : n + 16, :]
        hd[OFF + low : OFF + low + 16, :] = 0.5 - 0.5 * harmed_1[n : n + 16, :]

    def contact(b):
        return rows_of(ext.at[14], OFF, b)

    def spoil(row, b):
        old = rows_of(ext.at[12], OFF, b)
        new = harm(b, row, aver, rows_of(ext.at[13], OFF, b), old, hd, cover, decay)
        ext[12, OFF + b : OFF + b + 8, :] = new

    gather(ext, OFF, (-24, -8, 120, 136), energy, turned, band)
    for pair in range(6):
        aver[pair] = partial[pair] + row_sums(turned, pair, 64, rim_1, rim_2)
    for row, b in enumerate((*range(-16, 16, 8), *range(112, 144, 8))):
        spoil(8 * row, b)

    def put_next(k, b, value):
        ext2[k, OFF + b : OFF + b + 8, :] = value

    move(-16, 16, ext, OFF, hd, contact, rate, wp, fm, put_next)
    move(112, 144, ext, OFF, hd, contact, rate, wp, fm, put_next)

    gather(ext2, OFF, (-16, 0, 16, 96, 112, 128), energy, turned, band)
    for pair in range(6):
        aver[pair] = row_sums(turned, pair, 96, all_1, all_2)
    for row, b in enumerate((*range(-8, 24, 8), *range(104, 136, 8))):
        spoil(8 * row, b)
    ext[12, OFF + 24 : OFF + 104, :] = harmed_2[...]
    for low in (24, 96):
        hd[OFF + low : OFF + low + 8, :] = 0.5 - 0.5 * harmed_2[low - 24 : low - 16, :]
    copies = []

    def send(n, field, out):
        done[n] = field.T[PAD : PAD + CX, :]
        copy = pltpu.make_async_copy(done.at[n], out, sems.at[n])
        copy.start()
        copies.append(copy)

    send(12, ext[12, OFF : OFF + CY, :], out_d)

    def put_last(k, b, value):
        final[k, b : b + 8, :] = value

    move(0, 24, ext2, OFF, hd, contact, rate, wp, fm, put_last)
    move(104, CY, ext2, OFF, hd, contact, rate, wp, fm, put_last)
    for k in range(6):
        send(k, final[k], out_u.at[k])
        send(6 + k, final[6 + k], out_v.at[k])
    for copy in copies:
        copy.wait()


def tables(count_x, count_y):
    lane, row = jnp.arange(LANES), jnp.arange(SPAN)
    pos_x = lane + lax.axis_index("transit") * CX - PAD
    pos_y = row + lax.axis_index("lateral") * CY - EDGE
    in_x = (pos_x >= 0) & (pos_x < count_x)
    in_y = (pos_y >= 0) & (pos_y < count_y)

    def weight(offset, inside):
        dist = offset.astype(F32)
        return jnp.where((jnp.abs(offset) <= RADIUS) & inside, jnp.exp(-dist * dist / 32.0), 0.0)

    def parts(x):
        high = lax.reduce_precision(x, 8, 7)
        return high.astype(BF16), (x - high).astype(BF16)

    def beside(x, y):
        return jnp.concatenate([x, y], 1)

    along = weight(lane[:, None] - lane[None, :], in_x[:, None])
    across = weight(row[None, :] - row[:, None], in_y[None, :])
    cover = jnp.sum(across, 1)[:, None] * jnp.sum(along, 0)[None, :]
    inside = in_y[:, None] & in_x[None, :]
    cover = jnp.where(inside, cover, 1.0)
    decay = jnp.where(inside, -1.0 / (24.0 * cover), 0.0)
    rate = jnp.where(inside, DT, 0.0)
    high, low = parts(along)
    band = beside(high, low)
    band = jnp.concatenate([band, band], 0)
    own = (row > EDGE) & (row < EDGE + CY - 1)
    high, low = parts(jnp.where(own[None, :], across, 0.0)[16:176, EDGE : EDGE + CY])
    own_1, own_2 = beside(high, high), low
    outer = jnp.where(own[None, :], 0.0, across)

    def ends(x, n, m):
        return jnp.concatenate([x[EDGE - n : EDGE + m], x[EDGE + CY - m : EDGE + CY + n]], 0)

    high, low = parts(ends(ends(outer, 16, 16).T, 24, 8).T)
    rim_1, rim_2 = beside(high, high), low
    high, low = parts(ends(ends(across, 8, 24).T, 16, 32).T)
    all_1, all_2 = beside(high, high), low
    sure = (row >= EDGE + 11) & (row <= EDGE + 116)
    high, low = parts(jnp.where(sure[None, :], across, 0.0)[EDGE + 16 : EDGE + 112, EDGE + 8 : EDGE + 120])
    mid_1, mid_2 = beside(high, high), low
    maps = (4.0 * cover, decay, rate)
    return band, (own_1, own_2, mid_1, mid_2, *maps), (rim_1, rim_2, all_1, all_2, *maps)


def vmem(n):
    return [pl.BlockSpec(memory_space=pltpu.VMEM)] * n


def on_device(displacement, velocity, damage, strength, contact, flaw_cells):
    params = pltpu.CompilerParams(vmem_limit_bytes=48 * 1024 * 1024)
    shape = jax.ShapeDtypeStruct
    inputs = [
        pltpu.with_memory_space_constraint(x, pltpu.HBM)
        for x in (flaw_cells, displacement, velocity, damage, strength, contact)
    ]
    flaw_copy = pltpu.SMEM(flaw_cells.shape, jnp.int32)
    send_a, send_b = pl.pallas_call(
        pack_kernel,
        out_shape=[shape((SLAB, LANES), F32)] * 2,
        in_specs=[pl.BlockSpec(memory_space=pltpu.HBM)] * 6,
        out_specs=vmem(2),
        scratch_shapes=[
            pltpu.VMEM((2, 6, 24, CY), F32),
            pltpu.VMEM((2, 6, 16, CY), F32),
            pltpu.VMEM((2, 16, CY), F32),
            pltpu.VMEM((2, 16, CY), F32),
            pltpu.VMEM((2, 16, CY), jnp.int32),
            flaw_copy,
            pltpu.SemaphoreType.DMA((11,)),
        ],
        compiler_params=params,
        name="pack_rows",
    )(*inputs)
    got = swap((send_a, send_b), "transit")
    tile = shape((CX, CY), F32)
    own = pl.pallas_call(
        load_kernel,
        out_shape=[shape((6, CX, CY), F32)] * 2 + [tile, tile, shape((CX, CY), jnp.int32)],
        in_specs=[pl.BlockSpec(memory_space=pltpu.HBM)] * 6,
        out_specs=vmem(5),
        scratch_shapes=[pltpu.VMEM((CX, CY), F32), flaw_copy, pltpu.SemaphoreType.DMA((6,))],
        compiler_params=params,
        name="load_tile",
    )(*inputs)
    side_a, side_b, flat = pl.pallas_call(
        edge_kernel,
        out_shape=[shape((SLAB, LANES), F32)] * 2 + [shape((15, 16 + CY, LANES), F32)],
        in_specs=vmem(7),
        out_specs=vmem(3),
        scratch_shapes=[pltpu.VMEM((15, LANES, LANES), F32)],
        compiler_params=params,
        name="turn_and_cut",
    )(*own, *got)
    side = swap((side_a, side_b), "lateral")
    band, of_own, table = tables(CX * lax.axis_size("transit"), CY * lax.axis_size("lateral"))
    held = pltpu.VMEM((HELD, LANES), F32)
    inner = pl.pallas_call(
        inner_kernel,
        out_shape=[
            shape((6, 64, 2 * LANES), F32),
            shape((12, 48, LANES), F32),
            shape((32, LANES), F32),
            shape((12, 80, LANES), F32),
            shape((80, LANES), F32),
        ],
        in_specs=vmem(9),
        out_specs=vmem(5),
        scratch_shapes=[
            pltpu.VMEM((12, HELD, LANES), F32),
            pltpu.VMEM((12, CY, 2 * LANES), BF16),
            pltpu.VMEM((6, 2 * CY, 2 * LANES), BF16),
            pltpu.VMEM((6, 112, 2 * LANES), F32),
            pltpu.VMEM((112, LANES), F32),
            pltpu.VMEM((8, HELD, LANES), F32),
            pltpu.VMEM((6, HELD, LANES), F32),
            held,
        ],
        compiler_params=params,
        cost_estimate=pl.CostEstimate(flops=800_000_000, bytes_accessed=2_000_000, transcendentals=0),
        name="inner_rows",
    )(flat, band, *of_own)
    out = pl.pallas_call(
        step_kernel,
        out_shape=[shape((6, CX, CY), F32)] * 2 + [shape((CX, CY), F32)],
        in_specs=vmem(16),
        out_specs=[pl.BlockSpec(memory_space=pltpu.HBM)] * 3,
        scratch_shapes=[
            pltpu.VMEM((15, HELD, LANES), F32),
            pltpu.VMEM((12, HELD, LANES), F32),
            pltpu.VMEM((8, HELD, LANES), F32),
            pltpu.VMEM((6, HELD, LANES), F32),
            held,
            pltpu.VMEM((12, 96, 2 * LANES), BF16),
            pltpu.VMEM((6, 192, 2 * LANES), BF16),
            pltpu.VMEM((6, 64, 2 * LANES), F32),
            pltpu.VMEM((12, CY, LANES), F32),
            pltpu.VMEM((13, CX, CY), F32),
            pltpu.SemaphoreType.DMA((13,)),
        ],
        compiler_params=params,
        name="two_steps",
    )(flat, *inner, *side[::-1], band, *table)
    return tuple(out)


def solution(mesh):
    return jax.shard_map(
        on_device,
        mesh=mesh,
        in_specs=(
            P(None, "transit", "lateral"),
            P(None, "transit", "lateral"),
            P("transit", "lateral"),
            P("transit", "lateral"),
            P("transit", "lateral"),
            P("transit", "lateral", None),
        ),
        out_specs=(
            P(None, "transit", "lateral"),
            P(None, "transit", "lateral"),
            P("transit", "lateral"),
        ),
        check_vma=False,
    )
```

```python
import functools

import jax
import jax.numpy as jnp
from jax import lax
from jax.experimental import pallas as pl
from jax.experimental.pallas import tpu as pltpu
from jax.sharding import PartitionSpec as P

RADIUS = 8
CX, CY = 64, 128
WIDE, NEAR = 20, 11
PAD = 24
EDGE = 32
SPAN = CY + 2 * EDGE
OFF = EDGE + 8
HELD = CY + 2 * OFF
LANES = 128
GROUP = 3
SLAB = 224
K_STIFF = (1.0, 1.0, 0.0, 0.5, 0.5, 0.2)
VISCOUS = 0.2
KEEP = 0.95
DT = 0.4
ALONG = ((2, 3, 1.0, 0.8), (1, 5, 1.0, 0.3))
ACROSS = ((2, 4, 1.0, 0.8), (0, 5, -1.0, 0.3))
F32, BF16 = jnp.float32, jnp.bfloat16


def halo_of(field):
    return WIDE if field < 6 else NEAR


def slab_start(field):
    return WIDE * field if field < 6 else 6 * WIDE + NEAR * (field - 6)


def swap(block, axis):
    count = lax.axis_size(axis)
    out = []
    for first, part in zip((0, 1), block):
        pairs = []
        for i in range(first, count - 1, 2):
            pairs += [(i, i + 1), (i + 1, i)]
        out.append(lax.ppermute(part, axis, pairs))
    return out


def weakness(rows, flaw):
    row = lax.broadcasted_iota(jnp.int32, (rows, CY), 0)
    row = jnp.where(row < rows // 2, row, row + (CX - rows))
    node = row * CY + lax.broadcasted_iota(jnp.int32, (rows, CY), 1)
    mark = node == flaw[0, 0, 0]
    for j in range(1, flaw.shape[2]):
        mark = mark | (node == flaw[0, 0, j])
    return jnp.where(mark, 0.4, 1.0)


def run_copies(pairs, sems):
    copies = [pltpu.make_async_copy(src, dst, sems.at[n]) for n, (src, dst) in enumerate(pairs)]
    for copy in copies:
        copy.start()
    copies[0].wait()
    return copies[1:]


def pack_kernel(flaw_in, disp_in, vel_in, dam_in, stren_in, con_in, out_a, out_b, disp, vel, dam, stren, con, flaw, sems):
    pairs = [(flaw_in, flaw)]
    for side in range(2):
        wide = pl.ds(side * (CX - 24), 24)
        near = pl.ds(side * (CX - 16), 16)
        pairs.append((disp_in.at[:, wide, :], disp.at[side]))
        pairs.append((vel_in.at[:, near, :], vel.at[side]))
    pairs += [(dam_in, dam), (stren_in, stren), (con_in, con)]
    others = run_copies(pairs, sems)
    factor = weakness(32, flaw)
    for copy in others:
        copy.wait()
    limits = [stren[0:16, :] * factor[0:16], stren[CX - 16 :, :] * factor[16:32]]

    def fill(out, side):
        for k in range(15):
            width, start = halo_of(k), slab_start(k)
            held = 24 if k < 6 else 16
            rows = slice(held - width, held) if side else slice(0, width)
            if k < 6:
                part = disp[side, k, rows, :]
            elif k < 12:
                part = vel[side, k - 6, rows, :]
            elif k == 13:
                part = limits[side][rows, :]
            else:
                rows = slice(CX - width, CX) if side else rows
                part = (dam if k == 12 else con)[rows, :].astype(F32)
            out[start : start + width, :] = part
        out[219:SLAB, :] = jnp.zeros((SLAB - 219, LANES), F32)

    even = lax.rem(lax.axis_index("transit"), 2) == 0

    @pl.when(even)
    def _():
        fill(out_a, 1)
        fill(out_b, 0)

    @pl.when(jnp.logical_not(even))
    def _():
        fill(out_a, 0)
        fill(out_b, 1)


def load_kernel(flaw_in, disp_in, vel_in, dam_in, stren_in, con_in, disp, vel, dam, lim, con, stren, flaw, sems):
    others = run_copies(
        zip(
            (flaw_in, disp_in, vel_in, dam_in, stren_in, con_in),
            (flaw, disp, vel, dam, stren, con),
        ),
        sems,
    )
    factor = weakness(CX, flaw)
    for copy in others:
        copy.wait()
    lim[...] = stren[...] * factor


def edge_kernel(disp, vel, dam, lim, con, got_a, got_b, out_a, out_b, flat, ext):
    even = lax.rem(lax.axis_index("transit"), 2) == 0
    even_l = lax.rem(lax.axis_index("lateral"), 2) == 0
    for k in range(15):
        width, start = halo_of(k), slab_start(k)
        part_a = got_a[start : start + width, :]
        part_b = got_b[start : start + width, :]
        if k < 6:
            own = disp[k]
        elif k < 12:
            own = vel[k - 6]
        else:
            own = (dam, lim, con)[k - 12][...].astype(F32)
        low, high = PAD, PAD + CX
        ext[k, 0 : low - width, :] = jnp.zeros((low - width, LANES), F32)
        ext[k, low - width : low, :] = jnp.where(even, part_b, part_a)
        ext[k, low:high, :] = own
        ext[k, high : high + width, :] = jnp.where(even, part_a, part_b)
        ext[k, high + width : LANES, :] = jnp.zeros((LANES - high - width, LANES), F32)
        turned = ext[k].T
        flat[k, 8 : 8 + CY, :] = turned
        flat[k, 0:8, :] = jnp.zeros((8, LANES), F32)
        flat[k, 8 + CY : 16 + CY, :] = jnp.zeros((8, LANES), F32)
        right, left = turned[CY - width :, :], turned[:width, :]
        out_a[start : start + width, :] = jnp.where(even_l, right, left)
        out_b[start : start + width, :] = jnp.where(even_l, left, right)
    for out in (out_a, out_b):
        out[219:SLAB, :] = jnp.zeros((SLAB - 219, LANES), F32)


def split(x):
    high = x.astype(BF16)
    return high, (x - high.astype(F32)).astype(BF16)


def next_lane(x):
    return pltpu.roll(x, LANES - 1, 1)


def prev_lane(x):
    return pltpu.roll(x, 1, 1)


def products(get, put):
    c = [get(k, 0) for k in range(6)]
    x = [next_lane(c[k]) - prev_lane(c[k]) for k in range(5)]
    y = [get(k, 1) - get(k, -1) for k in range(5)]
    plane = (x[0], y[1], y[0] + x[1])
    bend = (x[3], y[4], y[3] + x[4])
    e7 = x[2] - 2.0 * c[3]
    e8 = y[2] - 2.0 * c[4]
    e9 = 0.5 * (x[1] - y[0]) - 2.0 * c[5]
    values = []
    for p, q in zip(plane, bend):
        values += [p * p, p * q, q * q]
    for ch, value in enumerate(values + [e7 * e7, e8 * e8, e9 * e9]):
        high, low = split(value)
        put(ch, slice(0, LANES), high)
        put(ch, slice(LANES, 2 * LANES), low)


def lane_sums(energy, turned, rows, band):
    for ch in range(12):
        both = jnp.dot(energy[ch, 0:rows, :], band[...], preferred_element_type=F32)
        high, low = split(both[:, :LANES] + both[:, LANES:])
        cols = slice(ch % 2 * LANES, (ch % 2 + 1) * LANES)
        turned[ch // 2, 0:rows, cols] = high
        turned[ch // 2, rows : 2 * rows, cols] = low


def block_sums(energy, turned, block, rows, band):
    both = jnp.dot(energy[block], band[...], preferred_element_type=F32)
    high, low = split(both[:, :LANES] + both[:, LANES:])
    for ch in range(12):
        cols = slice(ch % 2 * LANES, (ch % 2 + 1) * LANES)
        part = slice(16 * ch, 16 * ch + 16)
        turned[ch // 2, 16 * block : 16 * block + 16, cols] = high[part]
        turned[ch // 2, rows + 16 * block : rows + 16 * block + 16, cols] = low[part]


def row_sums(turned, pair, rows, first, second):
    return jnp.dot(first[...], turned[pair, 0 : 2 * rows, :], preferred_element_type=F32) + jnp.dot(
        second[...], turned[pair, 0:rows, :], preferred_element_type=F32
    )


def new_damage(mean, level, old, decay):
    driving = jnp.zeros((8, LANES), F32)
    for comp, threshold in enumerate((0.6, 0.6, 1.2)):
        p, q, r = (mean(3 * comp + n) for n in range(3))
        base = p - threshold * level
        for depth in (0.75, 0.25):
            centre = base + (depth * depth) * r
            swing = (2.0 * depth) * q
            driving += jnp.maximum(centre + swing, 0.0) + jnp.maximum(centre - swing, 0.0)
        if comp == 2:
            driving += jnp.maximum(r - level, 0.0)
    for ch, threshold in ((9, 1.5), (10, 1.5), (11, 1.2)):
        driving += jnp.maximum(mean(ch) - threshold * level, 0.0)
    return jnp.maximum(old, 1.0 - jnp.exp(driving * decay))


def fluxes(base, gammas, s, pairs):
    plus, minus = list(base), list(base)
    for gamma, (lead, turn, sign, stiff) in zip(gammas, pairs):
        plus[lead] = minus[lead] = base[lead] + (sign * stiff) * gamma
        half = (0.5 * stiff) * gamma
        plus[turn], minus[turn] = base[turn] + half, base[turn] - half
    out_p = [s * x for x in plus]
    return out_p, [out_p[k] if plus[k] is minus[k] else s * minus[k] for k in range(6)]


def move(f0, f1, state, off, hd, contact, rate, wp, fm, put):
    for b in range(f0 - 8, f1 + 8, 8):
        at = slice(OFF + b, OFF + b + 8)
        here = slice(off + b, off + b + 8)
        u = [state[k, here, :] for k in range(6)]
        for k in range(6):
            value = VISCOUS * state[6 + k, here, :]
            if K_STIFF[k] == 1.0:
                value = u[k] + value
            elif K_STIFF[k]:
                value = K_STIFF[k] * u[k] + value
            wp[k, at, :] = value
        for n, (lead, turn, sign, _) in enumerate(ACROSS):
            wp[6 + n, at, :] = sign * u[lead] - 0.5 * u[turn]
    for b in range(f0 - 8, f1, 8):
        at = slice(OFF + b, OFF + b + 8)
        nxt = slice(OFF + b + 1, OFF + b + 9)
        prv = slice(OFF + b - 1, OFF + b + 7)
        here = slice(off + b, off + b + 8)
        u = [state[k, here, :] for k in range(6)]
        w = [wp[k, at, :] for k in range(6)]
        h = hd[at, :]
        base = [wp[k, nxt, :] - w[k] for k in range(6)]
        gammas = [
            wp[6 + n, nxt, :] - (sign * u[lead] + 0.5 * u[turn])
            for n, (lead, turn, sign, _) in enumerate(ACROSS)
        ]
        plus, minus = fluxes(base, gammas, h + hd[nxt, :], ACROSS)
        for k in range(6):
            fm[k, at, :] = minus[k]
        if b < f0:
            continue
        total = [plus[k] - fm[k, prv, :] for k in range(6)]
        base = [next_lane(w[k]) - w[k] for k in range(6)]
        gammas = [
            next_lane(sign * u[lead] - 0.5 * u[turn]) - (sign * u[lead] + 0.5 * u[turn])
            for lead, turn, sign, _ in ALONG
        ]
        plus, minus = fluxes(base, gammas, h + next_lane(h), ALONG)
        total = [total[k] + plus[k] - prev_lane(minus[k]) for k in range(6)]
        dt = rate[EDGE + b : EDGE + b + 8, :]
        grip = 2.0 * contact(b)
        total[0] = total[0] + grip * (1.5 - u[0])
        total[2] = total[2] + grip * (-0.5 - u[2])
        for k in range(6):
            v_new = KEEP * state[6 + k, here, :] + dt * total[k]
            put(6 + k, b, v_new)
            put(k, b, u[k] + dt * v_new)


def rows_of(ref, off, b):
    return ref[off + b : off + b + 8, :]


def harm(b, row, aver, limit, old, hd, cover, decay):
    def mean(ch):
        return aver[ch // 2, row : row + 8, ch % 2 * LANES : (ch % 2 + 1) * LANES]

    tab = slice(EDGE + b, EDGE + b + 8)
    new = new_damage(mean, limit * cover[tab, :], old, decay[tab, :])
    hd[OFF + b : OFF + b + 8, :] = 0.5 - 0.5 * new
    return new


def gather(state, off, starts, energy, turned, band, by_block=False):
    for n, b in enumerate(starts):
        def get(k, shift):
            return state[k, off + b + shift : off + b + shift + 16, :]

        def put(ch, cols, value):
            if by_block:
                energy[n, 16 * ch : 16 * ch + 16, cols] = value
            else:
                energy[ch, 16 * n : 16 * n + 16, cols] = value

        products(get, put)
        if by_block:
            block_sums(energy, turned, n, 16 * len(starts), band)
    if not by_block:
        lane_sums(energy, turned, 16 * len(starts), band)


def inner_kernel(
    flat, band, first, second, mid_1, mid_2, cover, decay, rate,
    partial, moved, harmed_1, final, harmed_2,
    next_state, energy, turned, aver, old, wp, fm, hd,
):
    for low in (0, 120):
        hd[OFF + low : OFF + low + 8, :] = jnp.full((8, LANES), 0.5, F32)
        for k in range(6):
            next_state[k, OFF + low : OFF + low + 8, :] = jnp.zeros((8, LANES), F32)
    gather(flat, 8, range(0, CY, 16), energy, turned, band)
    for pair in range(6):
        sums = row_sums(turned, pair, CY, first, second)
        partial[pair, 0:32, :] = sums[0:32]
        aver[pair] = sums[24:136]
        partial[pair, 32:64, :] = sums[128:160]

    def contact(b):
        return rows_of(flat.at[14], 8, b)

    for b in range(8, 120, 8):
        new = harm(b, b - 8, aver, rows_of(flat.at[13], 8, b), rows_of(flat.at[12], 8, b), hd, cover, decay)
        old[b - 8 : b, :] = new
    harmed_1[0:16, :] = old[8:24, :]
    harmed_1[16:32, :] = old[88:104, :]

    def put_next(k, b, value):
        next_state[k, OFF + b : OFF + b + 8, :] = value

    move(8, 120, flat, 8, hd, contact, rate, wp, fm, put_next)
    for k in range(12):
        moved[k, 0:24, :] = next_state[k, OFF + 16 : OFF + 40, :]
        moved[k, 24:48, :] = next_state[k, OFF + 88 : OFF + 112, :]
    gather(next_state, OFF, range(8, 120, 16), energy, turned, band)
    for pair in range(6):
        aver[pair, 0:96, :] = row_sums(turned, pair, 112, mid_1, mid_2)
    for b in range(16, 112, 8):
        new = harm(b, b - 16, aver, rows_of(flat.at[13], 8, b), old[b - 8 : b, :], hd, cover, decay)
        if 24 <= b < 104:
            harmed_2[b - 24 : b - 16, :] = new

    def put_last(k, b, value):
        final[k, b - 24 : b - 16, :] = value

    move(24, 104, next_state, OFF, hd, contact, rate, wp, fm, put_last)


def step_kernel(
    flat, partial, moved, harmed_1, inner, harmed_2, side_b, side_a,
    band, rim_1, rim_2, all_1, all_2, cover, decay, rate,
    out_u, out_v, out_d,
    ext, ext2, wp, fm, hd, energy, turned, aver, final, done, sems,
):
    even = lax.rem(lax.axis_index("lateral"), 2) == 0
    for k in range(15):
        width, start = halo_of(k), slab_start(k)
        part_a = side_a[start : start + width, :]
        part_b = side_b[start : start + width, :]
        ext[k, OFF - EDGE : OFF - width, :] = jnp.zeros((EDGE - width, LANES), F32)
        ext[k, OFF - width : OFF, :] = jnp.where(even, part_b, part_a)
        for low, high in ((0, 24), (104, CY)):
            ext[k, OFF + low : OFF + high, :] = flat[k, 8 + low : 8 + high, :]
        ext[k, OFF + CY : OFF + CY + width, :] = jnp.where(even, part_a, part_b)
        ext[k, OFF + CY + width : OFF + CY + EDGE, :] = jnp.zeros((EDGE - width, LANES), F32)
    for low in (-24, 144):
        for k in range(6):
            ext2[k, OFF + low : OFF + low + 8, :] = jnp.zeros((8, LANES), F32)
        hd[OFF + low : OFF + low + 8, :] = jnp.full((8, LANES), 0.5, F32)
    for k in range(12):
        ext2[k, OFF + 16 : OFF + 40, :] = moved[k, 0:24, :]
        ext2[k, OFF + 88 : OFF + 112, :] = moved[k, 24:48, :]
        final[k, 24:104, :] = inner[k]
    for n, low in ((0, 16), (16, 96)):
        ext[12, OFF + low : OFF + low + 16, :] = harmed_1[n : n + 16, :]
        hd[OFF + low : OFF + low + 16, :] = 0.5 - 0.5 * harmed_1[n : n + 16, :]

    def contact(b):
        return rows_of(ext.at[14], OFF, b)

    def spoil(row, b):
        old = rows_of(ext.at[12], OFF, b)
        new = harm(b, row, aver, rows_of(ext.at[13], OFF, b), old, hd, cover, decay)
        ext[12, OFF + b : OFF + b + 8, :] = new

    gather(ext, OFF, (-24, -8, 120, 136), energy, turned, band, True)
    for pair in range(6):
        aver[pair] = partial[pair] + row_sums(turned, pair, 64, rim_1, rim_2)
    for row, b in enumerate((*range(-16, 16, 8), *range(112, 144, 8))):
        spoil(8 * row, b)

    def put_next(k, b, value):
        ext2[k, OFF + b : OFF + b + 8, :] = value

    move(-16, 16, ext, OFF, hd, contact, rate, wp, fm, put_next)
    move(112, 144, ext, OFF, hd, contact, rate, wp, fm, put_next)

    gather(ext2, OFF, (-16, 0, 16, 96, 112, 128), energy, turned, band, True)
    for pair in range(6):
        aver[pair] = row_sums(turned, pair, 96, all_1, all_2)
    for row, b in enumerate((*range(-8, 24, 8), *range(104, 136, 8))):
        spoil(8 * row, b)
    ext[12, OFF + 24 : OFF + 104, :] = harmed_2[...]
    for low in (24, 96):
        hd[OFF + low : OFF + low + 8, :] = 0.5 - 0.5 * harmed_2[low - 24 : low - 16, :]
    copies = []

    def send(start, fields, out):
        for n, field in enumerate(fields):
            done[start + n] = field.T[PAD : PAD + CX, :]
        copy = pltpu.make_async_copy(done.at[pl.ds(start, len(fields))], out, sems.at[len(copies)])
        copy.start()
        copies.append(copy)

    send(12, [ext[12, OFF : OFF + CY, :]], out_d)

    def put_last(k, b, value):
        final[k, b : b + 8, :] = value

    move(0, 24, ext2, OFF, hd, contact, rate, wp, fm, put_last)
    move(104, CY, ext2, OFF, hd, contact, rate, wp, fm, put_last)
    for start in range(0, 12, GROUP):
        out = out_u if start < 6 else out_v
        send(start, [final[start + n] for n in range(GROUP)], out.at[pl.ds(start % 6, GROUP)])
    for copy in copies:
        copy.wait()


def tables(count_x, count_y):
    lane, row = jnp.arange(LANES), jnp.arange(SPAN)
    pos_x = lane + lax.axis_index("transit") * CX - PAD
    pos_y = row + lax.axis_index("lateral") * CY - EDGE
    in_x = (pos_x >= 0) & (pos_x < count_x)
    in_y = (pos_y >= 0) & (pos_y < count_y)

    def weight(offset, inside):
        dist = offset.astype(F32)
        return jnp.where((jnp.abs(offset) <= RADIUS) & inside, jnp.exp(-dist * dist / 32.0), 0.0)

    def parts(x):
        high = lax.reduce_precision(x, 8, 7)
        return high.astype(BF16), (x - high).astype(BF16)

    def beside(x, y):
        return jnp.concatenate([x, y], 1)

    along = weight(lane[:, None] - lane[None, :], in_x[:, None])
    across = weight(row[None, :] - row[:, None], in_y[None, :])
    cover = jnp.sum(across, 1)[:, None] * jnp.sum(along, 0)[None, :]
    inside = in_y[:, None] & in_x[None, :]
    cover = jnp.where(inside, cover, 1.0)
    decay = jnp.where(inside, -1.0 / (24.0 * cover), 0.0)
    rate = jnp.where(inside, DT, 0.0)
    high, low = parts(along)
    band = beside(high, low)
    band = jnp.concatenate([band, band], 0)
    own = (row > EDGE) & (row < EDGE + CY - 1)
    high, low = parts(jnp.where(own[None, :], across, 0.0)[16:176, EDGE : EDGE + CY])
    own_1, own_2 = beside(high, high), low
    outer = jnp.where(own[None, :], 0.0, across)

    def ends(x, n, m):
        return jnp.concatenate([x[EDGE - n : EDGE + m], x[EDGE + CY - m : EDGE + CY + n]], 0)

    high, low = parts(ends(ends(outer, 16, 16).T, 24, 8).T)
    rim_1, rim_2 = beside(high, high), low
    high, low = parts(ends(ends(across, 8, 24).T, 16, 32).T)
    all_1, all_2 = beside(high, high), low
    sure = (row >= EDGE + 11) & (row <= EDGE + 116)
    high, low = parts(jnp.where(sure[None, :], across, 0.0)[EDGE + 16 : EDGE + 112, EDGE + 8 : EDGE + 120])
    mid_1, mid_2 = beside(high, high), low
    maps = (4.0 * cover, decay, rate)
    return band, (own_1, own_2, mid_1, mid_2, *maps), (rim_1, rim_2, all_1, all_2, *maps)


def vmem(n):
    return [pl.BlockSpec(memory_space=pltpu.VMEM)] * n


def on_device(displacement, velocity, damage, strength, contact, flaw_cells):
    params = pltpu.CompilerParams(vmem_limit_bytes=48 * 1024 * 1024)
    shape = jax.ShapeDtypeStruct
    inputs = [
        pltpu.with_memory_space_constraint(x, pltpu.HBM)
        for x in (flaw_cells, displacement, velocity, damage, strength, contact)
    ]
    flaw_copy = pltpu.SMEM(flaw_cells.shape, jnp.int32)
    send_a, send_b = pl.pallas_call(
        pack_kernel,
        out_shape=[shape((SLAB, LANES), F32)] * 2,
        in_specs=[pl.BlockSpec(memory_space=pltpu.HBM)] * 6,
        out_specs=vmem(2),
        scratch_shapes=[
            pltpu.VMEM((2, 6, 24, CY), F32),
            pltpu.VMEM((2, 6, 16, CY), F32),
            pltpu.VMEM((CX, CY), F32),
            pltpu.VMEM((CX, CY), F32),
            pltpu.VMEM((CX, CY), jnp.int32),
            flaw_copy,
            pltpu.SemaphoreType.DMA((8,)),
        ],
        compiler_params=params,
        name="pack_rows",
    )(*inputs)
    got = swap((send_a, send_b), "transit")
    tile = shape((CX, CY), F32)
    own = pl.pallas_call(
        load_kernel,
        out_shape=[shape((6, CX, CY), F32)] * 2 + [tile, tile, shape((CX, CY), jnp.int32)],
        in_specs=[pl.BlockSpec(memory_space=pltpu.HBM)] * 6,
        out_specs=vmem(5),
        scratch_shapes=[pltpu.VMEM((CX, CY), F32), flaw_copy, pltpu.SemaphoreType.DMA((6,))],
        compiler_params=params,
        name="load_tile",
    )(*inputs)
    side_a, side_b, flat = pl.pallas_call(
        edge_kernel,
        out_shape=[shape((SLAB, LANES), F32)] * 2 + [shape((15, 16 + CY, LANES), F32)],
        in_specs=vmem(7),
        out_specs=vmem(3),
        scratch_shapes=[pltpu.VMEM((15, LANES, LANES), F32)],
        compiler_params=params,
        name="turn_and_cut",
    )(*own, *got)
    side = swap((side_a, side_b), "lateral")
    band, of_own, table = tables(CX * lax.axis_size("transit"), CY * lax.axis_size("lateral"))
    held = pltpu.VMEM((HELD, LANES), F32)
    inner = pl.pallas_call(
        inner_kernel,
        out_shape=[
            shape((6, 64, 2 * LANES), F32),
            shape((12, 48, LANES), F32),
            shape((32, LANES), F32),
            shape((12, 80, LANES), F32),
            shape((80, LANES), F32),
        ],
        in_specs=vmem(9),
        out_specs=vmem(5),
        scratch_shapes=[
            pltpu.VMEM((12, HELD, LANES), F32),
            pltpu.VMEM((12, CY, 2 * LANES), BF16),
            pltpu.VMEM((6, 2 * CY, 2 * LANES), BF16),
            pltpu.VMEM((6, 112, 2 * LANES), F32),
            pltpu.VMEM((112, LANES), F32),
            pltpu.VMEM((8, HELD, LANES), F32),
            pltpu.VMEM((6, HELD, LANES), F32),
            held,
        ],
        compiler_params=params,
        cost_estimate=pl.CostEstimate(flops=800_000_000, bytes_accessed=2_000_000, transcendentals=0),
        name="inner_rows",
    )(flat, band, *of_own)
    out = pl.pallas_call(
        step_kernel,
        out_shape=[shape((6, CX, CY), F32)] * 2 + [shape((1, CX, CY), F32)],
        in_specs=vmem(16),
        out_specs=[pl.BlockSpec(memory_space=pltpu.HBM)] * 3,
        scratch_shapes=[
            pltpu.VMEM((15, HELD, LANES), F32),
            pltpu.VMEM((12, HELD, LANES), F32),
            pltpu.VMEM((8, HELD, LANES), F32),
            pltpu.VMEM((6, HELD, LANES), F32),
            held,
            pltpu.VMEM((6, 192, 2 * LANES), BF16),
            pltpu.VMEM((6, 192, 2 * LANES), BF16),
            pltpu.VMEM((6, 64, 2 * LANES), F32),
            pltpu.VMEM((12, CY, LANES), F32),
            pltpu.VMEM((13, CX, CY), F32),
            pltpu.SemaphoreType.DMA((13 // GROUP + 1,)),
        ],
        compiler_params=params,
        name="two_steps",
    )(flat, *inner, *side[::-1], band, *table)
    return out[0], out[1], out[2].reshape(CX, CY)


def solution(mesh):
    return jax.shard_map(
        on_device,
        mesh=mesh,
        in_specs=(
            P(None, "transit", "lateral"),
            P(None, "transit", "lateral"),
            P("transit", "lateral"),
            P("transit", "lateral"),
            P("transit", "lateral"),
            P("transit", "lateral", None),
        ),
        out_specs=(
            P(None, "transit", "lateral"),
            P(None, "transit", "lateral"),
            P("transit", "lateral"),
        ),
        check_vma=False,
    )
```

```python
import functools

import jax
import jax.numpy as jnp
from jax import lax
from jax.experimental import pallas as pl
from jax.experimental.pallas import tpu as pltpu
from jax.sharding import PartitionSpec as P

RADIUS = 8
CX, CY = 64, 128
WIDE, NEAR = 20, 11
PAD = 24
EDGE = 32
SPAN = CY + 2 * EDGE
OFF = EDGE + 8
HELD = CY + 2 * OFF
LANES = 128
GROUP = 3
SLAB = 224
K_STIFF = (1.0, 1.0, 0.0, 0.5, 0.5, 0.2)
VISCOUS = 0.2
KEEP = 0.95
DT = 0.4
ALONG = ((2, 3, 1.0, 0.8), (1, 5, 1.0, 0.3))
ACROSS = ((2, 4, 1.0, 0.8), (0, 5, -1.0, 0.3))
F32, BF16 = jnp.float32, jnp.bfloat16


def halo_of(field):
    return WIDE if field < 6 else NEAR


def slab_start(field):
    return WIDE * field if field < 6 else 6 * WIDE + NEAR * (field - 6)


def swap(block, axis):
    count = lax.axis_size(axis)
    out = []
    for first, part in zip((0, 1), block):
        pairs = []
        for i in range(first, count - 1, 2):
            pairs += [(i, i + 1), (i + 1, i)]
        out.append(lax.ppermute(part, axis, pairs))
    return out


def weakness(rows, flaw):
    row = lax.broadcasted_iota(jnp.int32, (rows, CY), 0)
    row = jnp.where(row < rows // 2, row, row + (CX - rows))
    node = row * CY + lax.broadcasted_iota(jnp.int32, (rows, CY), 1)
    mark = node == flaw[0, 0, 0]
    for j in range(1, flaw.shape[2]):
        mark = mark | (node == flaw[0, 0, j])
    return jnp.where(mark, 0.4, 1.0)


def run_copies(pairs, sems):
    copies = [pltpu.make_async_copy(src, dst, sems.at[n]) for n, (src, dst) in enumerate(pairs)]
    for copy in copies:
        copy.start()
    copies[0].wait()
    return copies[1:]


def pack_kernel(flaw_in, disp_in, vel_in, dam_in, stren_in, con_in, out_a, out_b, disp, vel, dam, stren, con, flaw, sems):
    pairs = [(flaw_in, flaw)]
    for side in range(2):
        wide = pl.ds(side * (CX - 24), 24)
        near = pl.ds(side * (CX - 16), 16)
        pairs.append((disp_in.at[:, wide, :], disp.at[side]))
        pairs.append((vel_in.at[:, near, :], vel.at[side]))
    pairs += [(dam_in, dam), (stren_in, stren), (con_in, con)]
    others = run_copies(pairs, sems)
    factor = weakness(32, flaw)
    for copy in others:
        copy.wait()
    limits = [stren[0:16, :] * factor[0:16], stren[CX - 16 :, :] * factor[16:32]]

    def fill(out, side):
        for k in range(15):
            width, start = halo_of(k), slab_start(k)
            held = 24 if k < 6 else 16
            rows = slice(held - width, held) if side else slice(0, width)
            if k < 6:
                part = disp[side, k, rows, :]
            elif k < 12:
                part = vel[side, k - 6, rows, :]
            elif k == 13:
                part = limits[side][rows, :]
            else:
                rows = slice(CX - width, CX) if side else rows
                part = (dam if k == 12 else con)[rows, :].astype(F32)
            out[start : start + width, :] = part
        out[219:SLAB, :] = jnp.zeros((SLAB - 219, LANES), F32)

    even = lax.rem(lax.axis_index("transit"), 2) == 0

    @pl.when(even)
    def _():
        fill(out_a, 1)
        fill(out_b, 0)

    @pl.when(jnp.logical_not(even))
    def _():
        fill(out_a, 0)
        fill(out_b, 1)


def load_kernel(flaw_in, disp_in, vel_in, dam_in, stren_in, con_in, own, disp, vel, dam, stren, con, flaw, sems):
    others = run_copies(
        zip(
            (flaw_in, disp_in, vel_in, dam_in, stren_in, con_in),
            (flaw, disp, vel, dam, stren, con),
        ),
        sems,
    )
    factor = weakness(CX, flaw)
    for copy in others:
        copy.wait()
    before, behind = jnp.zeros((PAD, CY), F32), jnp.zeros((LANES - PAD - CX, CY), F32)
    fields = [disp[k] for k in range(6)] + [vel[k] for k in range(6)]
    fields += [dam[...], stren[...] * factor, con[...].astype(F32)]
    for k, field in enumerate(fields):
        own[k] = jnp.concatenate([before, field, behind], 0).T


def turned_halo(got_a, got_b):
    even = lax.rem(lax.axis_index("transit"), 2) == 0
    lower, upper = [], []
    for rows in (slice(0, LANES), slice(SLAB - LANES, SLAB)):
        part_a, part_b = got_a[rows, :].T, got_b[rows, :].T
        lower.append(jnp.where(even, part_b, part_a))
        upper.append(jnp.where(even, part_a, part_b))
    return lower, upper


def with_halo(k, rows, own, halo):
    width, start = halo_of(k), slab_start(k)
    piece = int(start + width > LANES)
    start -= piece * (SLAB - LANES)
    lower, upper = (x[piece][rows, :] for x in halo)
    lane = lax.broadcasted_iota(jnp.int32, lower.shape, 1)
    lower = pltpu.roll(lower, (PAD - width - start) % LANES, 1)
    upper = pltpu.roll(upper, (PAD + CX - start) % LANES, 1)
    return jnp.where(lane < PAD, lower, jnp.where(lane < PAD + CX, own[k, rows, :], upper))


def edge_kernel(own, got_a, got_b, out_a, out_b):
    even = lax.rem(lax.axis_index("lateral"), 2) == 0
    halo = turned_halo(got_a, got_b)
    for k in range(15):
        width, start = halo_of(k), slab_start(k)
        held = 24 if k < 6 else 16
        left = with_halo(k, slice(0, held), own, halo)[:width]
        right = with_halo(k, slice(CY - held, CY), own, halo)[held - width :]
        out_a[start : start + width, :] = jnp.where(even, right, left)
        out_b[start : start + width, :] = jnp.where(even, left, right)
    for out in (out_a, out_b):
        out[219:SLAB, :] = jnp.zeros((SLAB - 219, LANES), F32)


def split(x):
    high = x.astype(BF16)
    return high, (x - high.astype(F32)).astype(BF16)


def next_lane(x):
    return pltpu.roll(x, LANES - 1, 1)


def prev_lane(x):
    return pltpu.roll(x, 1, 1)


def products(get, put):
    c = [get(k, 0) for k in range(6)]
    x = [next_lane(c[k]) - prev_lane(c[k]) for k in range(5)]
    y = [get(k, 1) - get(k, -1) for k in range(5)]
    plane = (x[0], y[1], y[0] + x[1])
    bend = (x[3], y[4], y[3] + x[4])
    e7 = x[2] - 2.0 * c[3]
    e8 = y[2] - 2.0 * c[4]
    e9 = 0.5 * (x[1] - y[0]) - 2.0 * c[5]
    values = []
    for p, q in zip(plane, bend):
        values += [p * p, p * q, q * q]
    for ch, value in enumerate(values + [e7 * e7, e8 * e8, e9 * e9]):
        high, low = split(value)
        put(ch, slice(0, LANES), high)
        put(ch, slice(LANES, 2 * LANES), low)


def lane_sums(energy, turned, rows, band):
    for ch in range(12):
        both = jnp.dot(energy[ch, 0:rows, :], band[...], preferred_element_type=F32)
        high, low = split(both[:, :LANES] + both[:, LANES:])
        cols = slice(ch % 2 * LANES, (ch % 2 + 1) * LANES)
        turned[ch // 2, 0:rows, cols] = high
        turned[ch // 2, rows : 2 * rows, cols] = low


def block_sums(energy, turned, block, rows, band):
    both = jnp.dot(energy[block], band[...], preferred_element_type=F32)
    high, low = split(both[:, :LANES] + both[:, LANES:])
    for ch in range(12):
        cols = slice(ch % 2 * LANES, (ch % 2 + 1) * LANES)
        part = slice(16 * ch, 16 * ch + 16)
        turned[ch // 2, 16 * block : 16 * block + 16, cols] = high[part]
        turned[ch // 2, rows + 16 * block : rows + 16 * block + 16, cols] = low[part]


def row_sums(turned, pair, rows, first, second):
    return jnp.dot(first[...], turned[pair, 0 : 2 * rows, :], preferred_element_type=F32) + jnp.dot(
        second[...], turned[pair, 0:rows, :], preferred_element_type=F32
    )


def new_damage(mean, level, old, decay):
    driving = jnp.zeros((8, LANES), F32)
    for comp, threshold in enumerate((0.6, 0.6, 1.2)):
        p, q, r = (mean(3 * comp + n) for n in range(3))
        base = p - threshold * level
        for depth in (0.75, 0.25):
            centre = base + (depth * depth) * r
            swing = (2.0 * depth) * q
            driving += jnp.maximum(centre + swing, 0.0) + jnp.maximum(centre - swing, 0.0)
        if comp == 2:
            driving += jnp.maximum(r - level, 0.0)
    for ch, threshold in ((9, 1.5), (10, 1.5), (11, 1.2)):
        driving += jnp.maximum(mean(ch) - threshold * level, 0.0)
    return jnp.maximum(old, 1.0 - jnp.exp(driving * decay))


def fluxes(base, gammas, s, pairs):
    plus, minus = list(base), list(base)
    for gamma, (lead, turn, sign, stiff) in zip(gammas, pairs):
        plus[lead] = minus[lead] = base[lead] + (sign * stiff) * gamma
        half = (0.5 * stiff) * gamma
        plus[turn], minus[turn] = base[turn] + half, base[turn] - half
    out_p = [s * x for x in plus]
    return out_p, [out_p[k] if plus[k] is minus[k] else s * minus[k] for k in range(6)]


def move(f0, f1, state, off, hd, contact, rate, wp, fm, put):
    for b in range(f0 - 8, f1 + 8, 8):
        at = slice(OFF + b, OFF + b + 8)
        here = slice(off + b, off + b + 8)
        u = [state[k, here, :] for k in range(6)]
        for k in range(6):
            value = VISCOUS * state[6 + k, here, :]
            if K_STIFF[k] == 1.0:
                value = u[k] + value
            elif K_STIFF[k]:
                value = K_STIFF[k] * u[k] + value
            wp[k, at, :] = value
        for n, (lead, turn, sign, _) in enumerate(ACROSS):
            wp[6 + n, at, :] = sign * u[lead] - 0.5 * u[turn]
    for b in range(f0 - 8, f1, 8):
        at = slice(OFF + b, OFF + b + 8)
        nxt = slice(OFF + b + 1, OFF + b + 9)
        prv = slice(OFF + b - 1, OFF + b + 7)
        here = slice(off + b, off + b + 8)
        u = [state[k, here, :] for k in range(6)]
        w = [wp[k, at, :] for k in range(6)]
        h = hd[at, :]
        base = [wp[k, nxt, :] - w[k] for k in range(6)]
        gammas = [
            wp[6 + n, nxt, :] - (sign * u[lead] + 0.5 * u[turn])
            for n, (lead, turn, sign, _) in enumerate(ACROSS)
        ]
        plus, minus = fluxes(base, gammas, h + hd[nxt, :], ACROSS)
        for k in range(6):
            fm[k, at, :] = minus[k]
        if b < f0:
            continue
        total = [plus[k] - fm[k, prv, :] for k in range(6)]
        base = [next_lane(w[k]) - w[k] for k in range(6)]
        gammas = [
            next_lane(sign * u[lead] - 0.5 * u[turn]) - (sign * u[lead] + 0.5 * u[turn])
            for lead, turn, sign, _ in ALONG
        ]
        plus, minus = fluxes(base, gammas, h + next_lane(h), ALONG)
        total = [total[k] + plus[k] - prev_lane(minus[k]) for k in range(6)]
        dt = rate[EDGE + b : EDGE + b + 8, :]
        grip = 2.0 * contact(b)
        total[0] = total[0] + grip * (1.5 - u[0])
        total[2] = total[2] + grip * (-0.5 - u[2])
        for k in range(6):
            v_new = KEEP * state[6 + k, here, :] + dt * total[k]
            put(6 + k, b, v_new)
            put(k, b, u[k] + dt * v_new)


def rows_of(ref, off, b):
    return ref[off + b : off + b + 8, :]


def harm(b, row, aver, limit, old, hd, cover, decay):
    def mean(ch):
        return aver[ch // 2, row : row + 8, ch % 2 * LANES : (ch % 2 + 1) * LANES]

    tab = slice(EDGE + b, EDGE + b + 8)
    new = new_damage(mean, limit * cover[tab, :], old, decay[tab, :])
    hd[OFF + b : OFF + b + 8, :] = 0.5 - 0.5 * new
    return new


def gather(state, off, starts, energy, turned, band, by_block=False):
    for n, b in enumerate(starts):
        def get(k, shift):
            return state[k, off + b + shift : off + b + shift + 16, :]

        def put(ch, cols, value):
            if by_block:
                energy[n, 16 * ch : 16 * ch + 16, cols] = value
            else:
                energy[ch, 16 * n : 16 * n + 16, cols] = value

        products(get, put)
        if by_block:
            block_sums(energy, turned, n, 16 * len(starts), band)
    if not by_block:
        lane_sums(energy, turned, 16 * len(starts), band)


def inner_kernel(
    own, got_a, got_b, band, first, second, mid_1, mid_2, cover, decay, rate,
    flat, partial, moved, harmed_1, final, harmed_2,
    next_state, energy, turned, aver, old, wp, fm, hd,
):
    halo = turned_halo(got_a, got_b)
    for k in range(15):
        flat[k, 0:8, :] = jnp.zeros((8, LANES), F32)
        flat[k, 8 : 8 + CY, :] = with_halo(k, slice(0, CY), own, halo)
        flat[k, 8 + CY : 16 + CY, :] = jnp.zeros((8, LANES), F32)
    for low in (0, 120):
        hd[OFF + low : OFF + low + 8, :] = jnp.full((8, LANES), 0.5, F32)
        for k in range(6):
            next_state[k, OFF + low : OFF + low + 8, :] = jnp.zeros((8, LANES), F32)
    gather(flat, 8, range(0, CY, 16), energy, turned, band)
    for pair in range(6):
        sums = row_sums(turned, pair, CY, first, second)
        partial[pair, 0:32, :] = sums[0:32]
        aver[pair] = sums[24:136]
        partial[pair, 32:64, :] = sums[128:160]

    def contact(b):
        return rows_of(flat.at[14], 8, b)

    for b in range(8, 120, 8):
        new = harm(b, b - 8, aver, rows_of(flat.at[13], 8, b), rows_of(flat.at[12], 8, b), hd, cover, decay)
        old[b - 8 : b, :] = new
    harmed_1[0:16, :] = old[8:24, :]
    harmed_1[16:32, :] = old[88:104, :]

    def put_next(k, b, value):
        next_state[k, OFF + b : OFF + b + 8, :] = value

    move(8, 120, flat, 8, hd, contact, rate, wp, fm, put_next)
    for k in range(12):
        moved[k, 0:24, :] = next_state[k, OFF + 16 : OFF + 40, :]
        moved[k, 24:48, :] = next_state[k, OFF + 88 : OFF + 112, :]
    gather(next_state, OFF, range(8, 120, 16), energy, turned, band)
    for pair in range(6):
        aver[pair, 0:96, :] = row_sums(turned, pair, 112, mid_1, mid_2)
    for b in range(16, 112, 8):
        new = harm(b, b - 16, aver, rows_of(flat.at[13], 8, b), old[b - 8 : b, :], hd, cover, decay)
        if 24 <= b < 104:
            harmed_2[b - 24 : b - 16, :] = new

    def put_last(k, b, value):
        final[k, b - 24 : b - 16, :] = value

    move(24, 104, next_state, OFF, hd, contact, rate, wp, fm, put_last)


def step_kernel(
    flat, partial, moved, harmed_1, inner, harmed_2, side_b, side_a,
    band, rim_1, rim_2, all_1, all_2, cover, decay, rate,
    out_u, out_v, out_d,
    ext, ext2, wp, fm, hd, energy, turned, aver, final, done, sems,
):
    even = lax.rem(lax.axis_index("lateral"), 2) == 0
    for k in range(15):
        width, start = halo_of(k), slab_start(k)
        part_a = side_a[start : start + width, :]
        part_b = side_b[start : start + width, :]
        ext[k, OFF - EDGE : OFF - width, :] = jnp.zeros((EDGE - width, LANES), F32)
        ext[k, OFF - width : OFF, :] = jnp.where(even, part_b, part_a)
        for low, high in ((0, 24), (104, CY)):
            ext[k, OFF + low : OFF + high, :] = flat[k, 8 + low : 8 + high, :]
        ext[k, OFF + CY : OFF + CY + width, :] = jnp.where(even, part_a, part_b)
        ext[k, OFF + CY + width : OFF + CY + EDGE, :] = jnp.zeros((EDGE - width, LANES), F32)
    for low in (-24, 144):
        for k in range(6):
            ext2[k, OFF + low : OFF + low + 8, :] = jnp.zeros((8, LANES), F32)
        hd[OFF + low : OFF + low + 8, :] = jnp.full((8, LANES), 0.5, F32)
    for k in range(12):
        ext2[k, OFF + 16 : OFF + 40, :] = moved[k, 0:24, :]
        ext2[k, OFF + 88 : OFF + 112, :] = moved[k, 24:48, :]
        final[k, 24:104, :] = inner[k]
    for n, low in ((0, 16), (16, 96)):
        ext[12, OFF + low : OFF + low + 16, :] = harmed_1[n : n + 16, :]
        hd[OFF + low : OFF + low + 16, :] = 0.5 - 0.5 * harmed_1[n : n + 16, :]

    def contact(b):
        return rows_of(ext.at[14], OFF, b)

    def spoil(row, b):
        old = rows_of(ext.at[12], OFF, b)
        new = harm(b, row, aver, rows_of(ext.at[13], OFF, b), old, hd, cover, decay)
        ext[12, OFF + b : OFF + b + 8, :] = new

    gather(ext, OFF, (-24, -8, 120, 136), energy, turned, band, True)
    for pair in range(6):
        aver[pair] = partial[pair] + row_sums(turned, pair, 64, rim_1, rim_2)
    for row, b in enumerate((*range(-16, 16, 8), *range(112, 144, 8))):
        spoil(8 * row, b)

    def put_next(k, b, value):
        ext2[k, OFF + b : OFF + b + 8, :] = value

    move(-16, 16, ext, OFF, hd, contact, rate, wp, fm, put_next)
    move(112, 144, ext, OFF, hd, contact, rate, wp, fm, put_next)

    gather(ext2, OFF, (-16, 0, 16, 96, 112, 128), energy, turned, band, True)
    for pair in range(6):
        aver[pair] = row_sums(turned, pair, 96, all_1, all_2)
    for row, b in enumerate((*range(-8, 24, 8), *range(104, 136, 8))):
        spoil(8 * row, b)
    ext[12, OFF + 24 : OFF + 104, :] = harmed_2[...]
    for low in (24, 96):
        hd[OFF + low : OFF + low + 8, :] = 0.5 - 0.5 * harmed_2[low - 24 : low - 16, :]
    copies = []

    def send(start, fields, out):
        for n, field in enumerate(fields):
            done[start + n] = field.T[PAD : PAD + CX, :]
        copy = pltpu.make_async_copy(done.at[pl.ds(start, len(fields))], out, sems.at[len(copies)])
        copy.start()
        copies.append(copy)

    send(12, [ext[12, OFF : OFF + CY, :]], out_d)

    def put_last(k, b, value):
        final[k, b : b + 8, :] = value

    move(0, 24, ext2, OFF, hd, contact, rate, wp, fm, put_last)
    move(104, CY, ext2, OFF, hd, contact, rate, wp, fm, put_last)
    for start in range(0, 12, GROUP):
        out = out_u if start < 6 else out_v
        send(start, [final[start + n] for n in range(GROUP)], out.at[pl.ds(start % 6, GROUP)])
    for copy in copies:
        copy.wait()


def tables(count_x, count_y):
    lane, row = jnp.arange(LANES), jnp.arange(SPAN)
    pos_x = lane + lax.axis_index("transit") * CX - PAD
    pos_y = row + lax.axis_index("lateral") * CY - EDGE
    in_x = (pos_x >= 0) & (pos_x < count_x)
    in_y = (pos_y >= 0) & (pos_y < count_y)

    def weight(offset, inside):
        dist = offset.astype(F32)
        return jnp.where((jnp.abs(offset) <= RADIUS) & inside, jnp.exp(-dist * dist / 32.0), 0.0)

    def parts(x):
        high = lax.reduce_precision(x, 8, 7)
        return high.astype(BF16), (x - high).astype(BF16)

    def beside(x, y):
        return jnp.concatenate([x, y], 1)

    along = weight(lane[:, None] - lane[None, :], in_x[:, None])
    across = weight(row[None, :] - row[:, None], in_y[None, :])
    cover = jnp.sum(across, 1)[:, None] * jnp.sum(along, 0)[None, :]
    inside = in_y[:, None] & in_x[None, :]
    cover = jnp.where(inside, cover, 1.0)
    decay = jnp.where(inside, -1.0 / (24.0 * cover), 0.0)
    rate = jnp.where(inside, DT, 0.0)
    high, low = parts(along)
    band = beside(high, low)
    band = jnp.concatenate([band, band], 0)
    own = (row > EDGE) & (row < EDGE + CY - 1)
    high, low = parts(jnp.where(own[None, :], across, 0.0)[16:176, EDGE : EDGE + CY])
    own_1, own_2 = beside(high, high), low
    outer = jnp.where(own[None, :], 0.0, across)

    def ends(x, n, m):
        return jnp.concatenate([x[EDGE - n : EDGE + m], x[EDGE + CY - m : EDGE + CY + n]], 0)

    high, low = parts(ends(ends(outer, 16, 16).T, 24, 8).T)
    rim_1, rim_2 = beside(high, high), low
    high, low = parts(ends(ends(across, 8, 24).T, 16, 32).T)
    all_1, all_2 = beside(high, high), low
    sure = (row >= EDGE + 11) & (row <= EDGE + 116)
    high, low = parts(jnp.where(sure[None, :], across, 0.0)[EDGE + 16 : EDGE + 112, EDGE + 8 : EDGE + 120])
    mid_1, mid_2 = beside(high, high), low
    maps = (4.0 * cover, decay, rate)
    return band, (own_1, own_2, mid_1, mid_2, *maps), (rim_1, rim_2, all_1, all_2, *maps)


def vmem(n):
    return [pl.BlockSpec(memory_space=pltpu.VMEM)] * n


def on_device(displacement, velocity, damage, strength, contact, flaw_cells):
    params = pltpu.CompilerParams(vmem_limit_bytes=48 * 1024 * 1024)
    shape = jax.ShapeDtypeStruct
    inputs = [
        pltpu.with_memory_space_constraint(x, pltpu.HBM)
        for x in (flaw_cells, displacement, velocity, damage, strength, contact)
    ]
    flaw_copy = pltpu.SMEM(flaw_cells.shape, jnp.int32)
    send_a, send_b = pl.pallas_call(
        pack_kernel,
        out_shape=[shape((SLAB, LANES), F32)] * 2,
        in_specs=[pl.BlockSpec(memory_space=pltpu.HBM)] * 6,
        out_specs=vmem(2),
        scratch_shapes=[
            pltpu.VMEM((2, 6, 24, CY), F32),
            pltpu.VMEM((2, 6, 16, CY), F32),
            pltpu.VMEM((CX, CY), F32),
            pltpu.VMEM((CX, CY), F32),
            pltpu.VMEM((CX, CY), jnp.int32),
            flaw_copy,
            pltpu.SemaphoreType.DMA((8,)),
        ],
        compiler_params=params,
        name="pack_rows",
    )(*inputs)
    got = swap((send_a, send_b), "transit")
    tile = pltpu.VMEM((CX, CY), F32)
    own = pl.pallas_call(
        load_kernel,
        out_shape=shape((15, CY, LANES), F32),
        in_specs=[pl.BlockSpec(memory_space=pltpu.HBM)] * 6,
        out_specs=vmem(1)[0],
        scratch_shapes=[
            pltpu.VMEM((6, CX, CY), F32),
            pltpu.VMEM((6, CX, CY), F32),
            tile,
            tile,
            pltpu.VMEM((CX, CY), jnp.int32),
            flaw_copy,
            pltpu.SemaphoreType.DMA((6,)),
        ],
        compiler_params=params,
        name="load_tile",
    )(*inputs)
    side = pl.pallas_call(
        edge_kernel,
        out_shape=[shape((SLAB, LANES), F32)] * 2,
        in_specs=vmem(3),
        out_specs=vmem(2),
        compiler_params=params,
        name="cut_columns",
    )(own, *got)
    side = swap(side, "lateral")
    band, of_own, table = tables(CX * lax.axis_size("transit"), CY * lax.axis_size("lateral"))
    held = pltpu.VMEM((HELD, LANES), F32)
    inner = pl.pallas_call(
        inner_kernel,
        out_shape=[
            shape((15, 16 + CY, LANES), F32),
            shape((6, 64, 2 * LANES), F32),
            shape((12, 48, LANES), F32),
            shape((32, LANES), F32),
            shape((12, 80, LANES), F32),
            shape((80, LANES), F32),
        ],
        in_specs=vmem(11),
        out_specs=vmem(6),
        scratch_shapes=[
            pltpu.VMEM((12, HELD, LANES), F32),
            pltpu.VMEM((12, CY, 2 * LANES), BF16),
            pltpu.VMEM((6, 2 * CY, 2 * LANES), BF16),
            pltpu.VMEM((6, 112, 2 * LANES), F32),
            pltpu.VMEM((112, LANES), F32),
            pltpu.VMEM((8, HELD, LANES), F32),
            pltpu.VMEM((6, HELD, LANES), F32),
            held,
        ],
        compiler_params=params,
        cost_estimate=pl.CostEstimate(flops=800_000_000, bytes_accessed=2_000_000, transcendentals=0),
        name="inner_rows",
    )(own, *got, band, *of_own)
    out = pl.pallas_call(
        step_kernel,
        out_shape=[shape((6, CX, CY), F32)] * 2 + [shape((1, CX, CY), F32)],
        in_specs=vmem(16),
        out_specs=[pl.BlockSpec(memory_space=pltpu.HBM)] * 3,
        scratch_shapes=[
            pltpu.VMEM((15, HELD, LANES), F32),
            pltpu.VMEM((12, HELD, LANES), F32),
            pltpu.VMEM((8, HELD, LANES), F32),
            pltpu.VMEM((6, HELD, LANES), F32),
            held,
            pltpu.VMEM((6, 192, 2 * LANES), BF16),
            pltpu.VMEM((6, 192, 2 * LANES), BF16),
            pltpu.VMEM((6, 64, 2 * LANES), F32),
            pltpu.VMEM((12, CY, LANES), F32),
            pltpu.VMEM((13, CX, CY), F32),
            pltpu.SemaphoreType.DMA((13 // GROUP + 1,)),
        ],
        compiler_params=params,
        name="two_steps",
    )(*inner, *side[::-1], band, *table)
    return out[0], out[1], out[2].reshape(CX, CY)


def solution(mesh):
    return jax.shard_map(
        on_device,
        mesh=mesh,
        in_specs=(
            P(None, "transit", "lateral"),
            P(None, "transit", "lateral"),
            P("transit", "lateral"),
            P("transit", "lateral"),
            P("transit", "lateral"),
            P("transit", "lateral", None),
        ),
        out_specs=(
            P(None, "transit", "lateral"),
            P(None, "transit", "lateral"),
            P("transit", "lateral"),
        ),
        check_vma=False,
    )
```

```python
import functools

import jax
import jax.numpy as jnp
from jax import lax
from jax.experimental import pallas as pl
from jax.experimental.pallas import tpu as pltpu
from jax.sharding import PartitionSpec as P

RADIUS = 8
CX, CY = 64, 128
WIDE, NEAR = 20, 11
PAD = 24
EDGE = 32
SPAN = CY + 2 * EDGE
OFF = EDGE + 8
HELD = CY + 2 * OFF
LANES = 128
SLAB = 224
K_STIFF = (1.0, 1.0, 0.0, 0.5, 0.5, 0.2)
VISCOUS = 0.2
KEEP = 0.95
DT = 0.4
ALONG = ((2, 3, 1.0, 0.8), (1, 5, 1.0, 0.3))
ACROSS = ((2, 4, 1.0, 0.8), (0, 5, -1.0, 0.3))
F32, BF16 = jnp.float32, jnp.bfloat16


def halo_of(field):
    return WIDE if field < 6 else NEAR


def slab_start(field):
    return WIDE * field if field < 6 else 6 * WIDE + NEAR * (field - 6)


def swap(block, axis):
    count = lax.axis_size(axis)
    out = []
    for first, part in block:
        pairs = []
        for i in range(first, count - 1, 2):
            pairs += [(i, i + 1), (i + 1, i)]
        out.append(lax.ppermute(part, axis, pairs))
    return out


def weakness(rows, flaw, first_row):
    node = lax.broadcasted_iota(jnp.int32, (rows, CY), 0) * CY + lax.broadcasted_iota(
        jnp.int32, (rows, CY), 1
    )
    mark = node == flaw[0, 0, 0] - first_row * CY
    for j in range(1, flaw.shape[2]):
        mark = mark | (node == flaw[0, 0, j] - first_row * CY)
    return jnp.where(mark, 0.4, 1.0)


def run_copies(pairs, sems):
    copies = [pltpu.make_async_copy(src, dst, sems.at[n]) for n, (src, dst) in enumerate(pairs)]
    for copy in copies:
        copy.start()
    copies[0].wait()
    return copies[1:]


def corner_place(k):
    if k < 6:
        return WIDE * (k // 3), 2 * WIDE * (k % 3)
    return 2 * WIDE + NEAR * ((k - 6) // 5), 2 * NEAR * ((k - 6) % 5)


def edge_rows(k, side, disp, vel, dam, lim, con):
    width = halo_of(k)
    rows = slice(CX - width, CX) if side else slice(0, width)
    if k < 6:
        return disp[k, rows, :]
    if k < 12:
        return vel[k - 6, rows, :]
    return (dam, lim, con)[k - 12][rows, :].astype(F32)


def fill(out, side, own):
    for k in range(15):
        out[slab_start(k) : slab_start(k) + halo_of(k), :] = edge_rows(k, side, *own)
    out[219:SLAB, :] = jnp.zeros((SLAB - 219, LANES), F32)


def on_parity(action):
    odd = lax.rem(lax.axis_index("transit"), 2) == 1

    @pl.when(odd)
    def _():
        action(1)

    @pl.when(jnp.logical_not(odd))
    def _():
        action(0)


def load_kernel(
    flaw_in, disp_in, vel_in, dam_in, stren_in, con_in, out_a, disp, vel, dam, lim, con, stren, flaw, sems
):
    others = run_copies(
        zip((flaw_in, disp_in, vel_in, dam_in, stren_in, con_in), (flaw, disp, vel, dam, stren, con)),
        sems,
    )
    factor = weakness(CX, flaw, 0)
    for copy in others:
        copy.wait()
    lim[...] = stren[...] * factor
    on_parity(lambda side: fill(out_a, side, (disp, vel, dam, lim, con)))


def near_kernel(disp, vel, dam, lim, con, corner, out_b):
    own = (disp, vel, dam, lim, con)

    def action(a_above):
        side = 1 - a_above
        for first, last in ((0, 3), (3, 6), (6, 11), (11, 15)):
            width = halo_of(first)
            lane = lax.broadcasted_iota(jnp.int32, (width, LANES), 1)
            block = jnp.zeros((width, LANES), F32)
            for k in range(first, last):
                row, start = corner_place(k)
                moved = pltpu.roll(edge_rows(k, side, *own), width + start, 1)
                block = jnp.where((lane >= start) & (lane < start + 2 * width), moved, block)
            corner[row : row + width, :] = block
        corner[62:64, :] = jnp.zeros((2, LANES), F32)
        fill(out_b, side, own)

    on_parity(action)


def own_field(k, disp, vel, dam, lim, con):
    if k < 6:
        return disp[k]
    if k < 12:
        return vel[k - 6]
    return (dam, lim, con)[k - 12][...].astype(F32)


def stack_rows(ext, k, part_a, part_b, own, even):
    width = halo_of(k)
    low, high = PAD, PAD + CX
    ext[k, 0 : low - width, :] = jnp.zeros((low - width, LANES), F32)
    ext[k, low - width : low, :] = jnp.where(even, part_b, part_a)
    ext[k, low:high, :] = own
    ext[k, high : high + width, :] = jnp.where(even, part_a, part_b)
    ext[k, high + width : LANES, :] = jnp.zeros((LANES - high - width, LANES), F32)


def turn_tile_kernel(disp, vel, dam, lim, con, own):
    before, behind = jnp.zeros((PAD, CY), F32), jnp.zeros((LANES - PAD - CX, CY), F32)
    for k in range(15):
        own[k] = jnp.concatenate([before, own_field(k, disp, vel, dam, lim, con), behind], 0).T


def cut_kernel(own, got_a, corner, out_a, out_b):
    even = lax.rem(lax.axis_index("lateral"), 2) == 0
    rows_a = [got_a[rows, :].T for rows in (slice(0, LANES), slice(SLAB - LANES, SLAB))]
    ends_b = jnp.concatenate([corner[...], corner[...]], 0).T

    def action(a_above):
        for k in range(15):
            width, start = halo_of(k), slab_start(k)
            piece = int(start + width > LANES)
            lane_a = start - piece * (SLAB - LANES)
            lane_b, place_b = corner_place(k)
            lane = lax.broadcasted_iota(jnp.int32, (width, LANES), 1)
            spots = [(PAD - width, lane < PAD), (PAD + CX, lane >= PAD + CX)]
            (spot_b, of_b), (spot_a, of_a) = spots if a_above else spots[::-1]
            found = []
            for rows, first in ((slice(CY - width, CY), place_b), (slice(0, width), place_b + width)):
                from_a = pltpu.roll(rows_a[piece][rows, :], (spot_a - lane_a) % LANES, 1)
                from_b = pltpu.roll(ends_b[first : first + width, :], (spot_b - lane_b) % LANES, 1)
                found.append(jnp.where(of_a, from_a, jnp.where(of_b, from_b, own[k, rows, :])))
            right, left = found
            out_a[start : start + width, :] = jnp.where(even, right, left)
            out_b[start : start + width, :] = jnp.where(even, left, right)

    on_parity(action)
    for out in (out_a, out_b):
        out[219:SLAB, :] = jnp.zeros((SLAB - 219, LANES), F32)


def turn_kernel(disp, vel, dam, lim, con, got_a, got_b, flat, ext):
    even = lax.rem(lax.axis_index("transit"), 2) == 1
    for k in range(15):
        rows = slice(slab_start(k), slab_start(k) + halo_of(k))
        own = own_field(k, disp, vel, dam, lim, con)
        stack_rows(ext, k, got_a[rows, :], got_b[rows, :], own, even)
        flat[k, 8 : 8 + CY, :] = ext[k].T
        flat[k, 0:8, :] = jnp.zeros((8, LANES), F32)
        flat[k, 8 + CY : 16 + CY, :] = jnp.zeros((8, LANES), F32)


def split(x):
    high = x.astype(BF16)
    return high, (x - high.astype(F32)).astype(BF16)


def next_lane(x):
    return pltpu.roll(x, LANES - 1, 1)


def prev_lane(x):
    return pltpu.roll(x, 1, 1)


def products(get, put):
    c = [get(k, 0) for k in range(6)]
    x = [next_lane(c[k]) - prev_lane(c[k]) for k in range(5)]
    y = [get(k, 1) - get(k, -1) for k in range(5)]
    plane = (x[0], y[1], y[0] + x[1])
    bend = (x[3], y[4], y[3] + x[4])
    e7 = x[2] - 2.0 * c[3]
    e8 = y[2] - 2.0 * c[4]
    e9 = 0.5 * (x[1] - y[0]) - 2.0 * c[5]
    values = []
    for p, q in zip(plane, bend):
        values += [p * p, p * q, q * q]
    for ch, value in enumerate(values + [e7 * e7, e8 * e8, e9 * e9]):
        high, low = split(value)
        put(ch, slice(0, LANES), high)
        put(ch, slice(LANES, 2 * LANES), low)


def lane_sums(energy, turned, rows, band):
    for ch in range(12):
        both = jnp.dot(energy[ch, 0:rows, :], band[...], preferred_element_type=F32)
        high, low = split(both[:, :LANES] + both[:, LANES:])
        cols = slice(ch % 2 * LANES, (ch % 2 + 1) * LANES)
        turned[ch // 2, 0:rows, cols] = high
        turned[ch // 2, rows : 2 * rows, cols] = low


def block_sums(energy, turned, block, rows, band):
    both = jnp.dot(energy[block], band[...], preferred_element_type=F32)
    high, low = split(both[:, :LANES] + both[:, LANES:])
    for ch in range(12):
        cols = slice(ch % 2 * LANES, (ch % 2 + 1) * LANES)
        part = slice(16 * ch, 16 * ch + 16)
        turned[ch // 2, 16 * block : 16 * block + 16, cols] = high[part]
        turned[ch // 2, rows + 16 * block : rows + 16 * block + 16, cols] = low[part]


def row_sums(turned, pair, rows, first, second):
    return jnp.dot(first[...], turned[pair, 0 : 2 * rows, :], preferred_element_type=F32) + jnp.dot(
        second[...], turned[pair, 0:rows, :], preferred_element_type=F32
    )


def new_damage(mean, level, old, decay):
    driving = jnp.zeros((8, LANES), F32)
    for comp, threshold in enumerate((0.6, 0.6, 1.2)):
        p, q, r = (mean(3 * comp + n) for n in range(3))
        base = p - threshold * level
        for depth in (0.75, 0.25):
            centre = base + (depth * depth) * r
            swing = (2.0 * depth) * q
            driving += jnp.maximum(centre + swing, 0.0) + jnp.maximum(centre - swing, 0.0)
        if comp == 2:
            driving += jnp.maximum(r - level, 0.0)
    for ch, threshold in ((9, 1.5), (10, 1.5), (11, 1.2)):
        driving += jnp.maximum(mean(ch) - threshold * level, 0.0)
    return jnp.maximum(old, 1.0 - jnp.exp(driving * decay))


def fluxes(base, gammas, s, pairs):
    plus, minus = list(base), list(base)
    for gamma, (lead, turn, sign, stiff) in zip(gammas, pairs):
        plus[lead] = minus[lead] = base[lead] + (sign * stiff) * gamma
        half = (0.5 * stiff) * gamma
        plus[turn], minus[turn] = base[turn] + half, base[turn] - half
    out_p = [s * x for x in plus]
    return out_p, [out_p[k] if plus[k] is minus[k] else s * minus[k] for k in range(6)]


def move(f0, f1, state, off, hd, contact, rate, wp, fm, put):
    for b in range(f0 - 8, f1 + 8, 8):
        at = slice(OFF + b, OFF + b + 8)
        here = slice(off + b, off + b + 8)
        u = [state[k, here, :] for k in range(6)]
        for k in range(6):
            value = VISCOUS * state[6 + k, here, :]
            if K_STIFF[k] == 1.0:
                value = u[k] + value
            elif K_STIFF[k]:
                value = K_STIFF[k] * u[k] + value
            wp[k, at, :] = value
        for n, (lead, turn, sign, _) in enumerate(ACROSS):
            wp[6 + n, at, :] = sign * u[lead] - 0.5 * u[turn]
    for b in range(f0 - 8, f1, 8):
        at = slice(OFF + b, OFF + b + 8)
        nxt = slice(OFF + b + 1, OFF + b + 9)
        prv = slice(OFF + b - 1, OFF + b + 7)
        here = slice(off + b, off + b + 8)
        u = [state[k, here, :] for k in range(6)]
        w = [wp[k, at, :] for k in range(6)]
        h = hd[at, :]
        base = [wp[k, nxt, :] - w[k] for k in range(6)]
        gammas = [
            wp[6 + n, nxt, :] - (sign * u[lead] + 0.5 * u[turn])
            for n, (lead, turn, sign, _) in enumerate(ACROSS)
        ]
        plus, minus = fluxes(base, gammas, h + hd[nxt, :], ACROSS)
        for k in range(6):
            fm[k, at, :] = minus[k]
        if b < f0:
            continue
        total = [plus[k] - fm[k, prv, :] for k in range(6)]
        base = [next_lane(w[k]) - w[k] for k in range(6)]
        gammas = [
            next_lane(sign * u[lead] - 0.5 * u[turn]) - (sign * u[lead] + 0.5 * u[turn])
            for lead, turn, sign, _ in ALONG
        ]
        plus, minus = fluxes(base, gammas, h + next_lane(h), ALONG)
        total = [total[k] + plus[k] - prev_lane(minus[k]) for k in range(6)]
        dt = rate[EDGE + b : EDGE + b + 8, :]
        grip = 2.0 * contact(b)
        total[0] = total[0] + grip * (1.5 - u[0])
        total[2] = total[2] + grip * (-0.5 - u[2])
        for k in range(6):
            v_new = KEEP * state[6 + k, here, :] + dt * total[k]
            put(6 + k, b, v_new)
            put(k, b, u[k] + dt * v_new)


def rows_of(ref, off, b):
    return ref[off + b : off + b + 8, :]


def harm(b, row, aver, limit, old, hd, cover, decay):
    def mean(ch):
        return aver[ch // 2, row : row + 8, ch % 2 * LANES : (ch % 2 + 1) * LANES]

    tab = slice(EDGE + b, EDGE + b + 8)
    new = new_damage(mean, limit * cover[tab, :], old, decay[tab, :])
    hd[OFF + b : OFF + b + 8, :] = 0.5 - 0.5 * new
    return new


def gather(state, off, starts, energy, turned, band, by_block=False):
    for n, b in enumerate(starts):
        def get(k, shift):
            return state[k, off + b + shift : off + b + shift + 16, :]

        def put(ch, cols, value):
            if by_block:
                energy[n, 16 * ch : 16 * ch + 16, cols] = value
            else:
                energy[ch, 16 * n : 16 * n + 16, cols] = value

        products(get, put)
        if by_block:
            block_sums(energy, turned, n, 16 * len(starts), band)
    if not by_block:
        lane_sums(energy, turned, 16 * len(starts), band)


def inner_kernel(
    flat, band, first, second, mid_1, mid_2, cover, decay, rate,
    partial, moved, harmed_1, final, harmed_2,
    next_state, energy, turned, aver, old, wp, fm, hd,
):
    for low in (0, 120):
        hd[OFF + low : OFF + low + 8, :] = jnp.full((8, LANES), 0.5, F32)
        for k in range(6):
            next_state[k, OFF + low : OFF + low + 8, :] = jnp.zeros((8, LANES), F32)
    gather(flat, 8, range(0, CY, 16), energy, turned, band)
    for pair in range(6):
        sums = row_sums(turned, pair, CY, first, second)
        partial[pair, 0:32, :] = sums[0:32]
        aver[pair] = sums[24:136]
        partial[pair, 32:64, :] = sums[128:160]

    def contact(b):
        return rows_of(flat.at[14], 8, b)

    for b in range(8, 120, 8):
        new = harm(b, b - 8, aver, rows_of(flat.at[13], 8, b), rows_of(flat.at[12], 8, b), hd, cover, decay)
        old[b - 8 : b, :] = new
    harmed_1[0:16, :] = old[8:24, :]
    harmed_1[16:32, :] = old[88:104, :]

    def put_next(k, b, value):
        next_state[k, OFF + b : OFF + b + 8, :] = value

    move(8, 120, flat, 8, hd, contact, rate, wp, fm, put_next)
    for k in range(12):
        moved[k, 0:24, :] = next_state[k, OFF + 16 : OFF + 40, :]
        moved[k, 24:48, :] = next_state[k, OFF + 88 : OFF + 112, :]
    gather(next_state, OFF, range(8, 120, 16), energy, turned, band)
    for pair in range(6):
        aver[pair, 0:96, :] = row_sums(turned, pair, 112, mid_1, mid_2)
    for b in range(16, 112, 8):
        new = harm(b, b - 16, aver, rows_of(flat.at[13], 8, b), old[b - 8 : b, :], hd, cover, decay)
        if 24 <= b < 104:
            harmed_2[b - 24 : b - 16, :] = new

    def put_last(k, b, value):
        final[k, b - 24 : b - 16, :] = value

    move(24, 104, next_state, OFF, hd, contact, rate, wp, fm, put_last)


def step_kernel(
    flat, partial, moved, harmed_1, inner, harmed_2, side_b, side_a,
    band, rim_1, rim_2, all_1, all_2, cover, decay, rate,
    out_u, out_v, out_d,
    ext, ext2, wp, fm, hd, energy, turned, aver, final, done, sems,
):
    even = lax.rem(lax.axis_index("lateral"), 2) == 0
    for k in range(15):
        width, start = halo_of(k), slab_start(k)
        part_a = side_a[start : start + width, :]
        part_b = side_b[start : start + width, :]
        ext[k, OFF - EDGE : OFF - width, :] = jnp.zeros((EDGE - width, LANES), F32)
        ext[k, OFF - width : OFF, :] = jnp.where(even, part_b, part_a)
        for low, high in ((0, 24), (104, CY)):
            ext[k, OFF + low : OFF + high, :] = flat[k, 8 + low : 8 + high, :]
        ext[k, OFF + CY : OFF + CY + width, :] = jnp.where(even, part_a, part_b)
        ext[k, OFF + CY + width : OFF + CY + EDGE, :] = jnp.zeros((EDGE - width, LANES), F32)
    for low in (-24, 144):
        for k in range(6):
            ext2[k, OFF + low : OFF + low + 8, :] = jnp.zeros((8, LANES), F32)
        hd[OFF + low : OFF + low + 8, :] = jnp.full((8, LANES), 0.5, F32)
    for k in range(12):
        ext2[k, OFF + 16 : OFF + 40, :] = moved[k, 0:24, :]
        ext2[k, OFF + 88 : OFF + 112, :] = moved[k, 24:48, :]
        final[k, 24:104, :] = inner[k]
    for n, low in ((0, 16), (16, 96)):
        ext[12, OFF + low : OFF + low + 16, :] = harmed_1[n : n + 16, :]
        hd[OFF + low : OFF + low + 16, :] = 0.5 - 0.5 * harmed_1[n : n + 16, :]

    def contact(b):
        return rows_of(ext.at[14], OFF, b)

    def spoil(row, b):
        old = rows_of(ext.at[12], OFF, b)
        new = harm(b, row, aver, rows_of(ext.at[13], OFF, b), old, hd, cover, decay)
        ext[12, OFF + b : OFF + b + 8, :] = new

    gather(ext, OFF, (-24, -8, 120, 136), energy, turned, band, True)
    for pair in range(6):
        aver[pair] = partial[pair] + row_sums(turned, pair, 64, rim_1, rim_2)
    for row, b in enumerate((*range(-16, 16, 8), *range(112, 144, 8))):
        spoil(8 * row, b)

    def put_next(k, b, value):
        ext2[k, OFF + b : OFF + b + 8, :] = value

    move(-16, 16, ext, OFF, hd, contact, rate, wp, fm, put_next)
    move(112, 144, ext, OFF, hd, contact, rate, wp, fm, put_next)

    gather(ext2, OFF, (-16, 0, 16, 96, 112, 128), energy, turned, band, True)
    for pair in range(6):
        aver[pair] = row_sums(turned, pair, 96, all_1, all_2)
    for row, b in enumerate((*range(-8, 24, 8), *range(104, 136, 8))):
        spoil(8 * row, b)
    ext[12, OFF + 24 : OFF + 104, :] = harmed_2[...]
    for low in (24, 96):
        hd[OFF + low : OFF + low + 8, :] = 0.5 - 0.5 * harmed_2[low - 24 : low - 16, :]
    copies = []

    def send(n, field, out):
        done[n] = field.T[PAD : PAD + CX, :]
        copy = pltpu.make_async_copy(done.at[n], out, sems.at[n])
        copy.start()
        copies.append(copy)

    send(12, ext[12, OFF : OFF + CY, :], out_d)

    def put_last(k, b, value):
        final[k, b : b + 8, :] = value

    move(0, 24, ext2, OFF, hd, contact, rate, wp, fm, put_last)
    move(104, CY, ext2, OFF, hd, contact, rate, wp, fm, put_last)
    for k in range(6):
        send(k, final[k], out_u.at[k])
        send(6 + k, final[6 + k], out_v.at[k])
    for copy in copies:
        copy.wait()


def tables(count_x, count_y):
    lane, row = jnp.arange(LANES), jnp.arange(SPAN)
    pos_x = lane + lax.axis_index("transit") * CX - PAD
    pos_y = row + lax.axis_index("lateral") * CY - EDGE
    in_x = (pos_x >= 0) & (pos_x < count_x)
    in_y = (pos_y >= 0) & (pos_y < count_y)

    def weight(offset, inside):
        dist = offset.astype(F32)
        return jnp.where((jnp.abs(offset) <= RADIUS) & inside, jnp.exp(-dist * dist / 32.0), 0.0)

    def parts(x):
        high = lax.reduce_precision(x, 8, 7)
        return high.astype(BF16), (x - high).astype(BF16)

    def beside(x, y):
        return jnp.concatenate([x, y], 1)

    along = weight(lane[:, None] - lane[None, :], in_x[:, None])
    across = weight(row[None, :] - row[:, None], in_y[None, :])
    cover = jnp.sum(across, 1)[:, None] * jnp.sum(along, 0)[None, :]
    inside = in_y[:, None] & in_x[None, :]
    cover = jnp.where(inside, cover, 1.0)
    decay = jnp.where(inside, -1.0 / (24.0 * cover), 0.0)
    rate = jnp.where(inside, DT, 0.0)
    high, low = parts(along)
    band = beside(high, low)
    band = jnp.concatenate([band, band], 0)
    own = (row > EDGE) & (row < EDGE + CY - 1)
    high, low = parts(jnp.where(own[None, :], across, 0.0)[16:176, EDGE : EDGE + CY])
    own_1, own_2 = beside(high, high), low
    outer = jnp.where(own[None, :], 0.0, across)

    def ends(x, n, m):
        return jnp.concatenate([x[EDGE - n : EDGE + m], x[EDGE + CY - m : EDGE + CY + n]], 0)

    high, low = parts(ends(ends(outer, 16, 16).T, 24, 8).T)
    rim_1, rim_2 = beside(high, high), low
    high, low = parts(ends(ends(across, 8, 24).T, 16, 32).T)
    all_1, all_2 = beside(high, high), low
    sure = (row >= EDGE + 11) & (row <= EDGE + 116)
    high, low = parts(jnp.where(sure[None, :], across, 0.0)[EDGE + 16 : EDGE + 112, EDGE + 8 : EDGE + 120])
    mid_1, mid_2 = beside(high, high), low
    maps = (4.0 * cover, decay, rate)
    return band, (own_1, own_2, mid_1, mid_2, *maps), (rim_1, rim_2, all_1, all_2, *maps)


def vmem(n):
    return [pl.BlockSpec(memory_space=pltpu.VMEM)] * n


def on_device(displacement, velocity, damage, strength, contact, flaw_cells):
    params = pltpu.CompilerParams(vmem_limit_bytes=48 * 1024 * 1024)
    shape = jax.ShapeDtypeStruct
    inputs = [
        pltpu.with_memory_space_constraint(x, pltpu.HBM)
        for x in (flaw_cells, displacement, velocity, damage, strength, contact)
    ]
    tile = shape((CX, CY), F32)
    send_a, *own = pl.pallas_call(
        load_kernel,
        out_shape=[shape((SLAB, LANES), F32)]
        + [shape((6, CX, CY), F32)] * 2
        + [tile, tile, shape((CX, CY), jnp.int32)],
        in_specs=[pl.BlockSpec(memory_space=pltpu.HBM)] * 6,
        out_specs=vmem(6),
        scratch_shapes=[
            pltpu.VMEM((CX, CY), F32),
            pltpu.SMEM(flaw_cells.shape, jnp.int32),
            pltpu.SemaphoreType.DMA((6,)),
        ],
        compiler_params=params,
        name="load_tile",
    )(*inputs)
    corner, send_b = pl.pallas_call(
        near_kernel,
        out_shape=[shape((64, LANES), F32), shape((SLAB, LANES), F32)],
        in_specs=vmem(5),
        out_specs=vmem(2),
        compiler_params=params,
        name="near_rows",
    )(*own)
    got_a, got_corner, got_b = swap(((1, send_a), (0, corner), (0, send_b)), "transit")
    fields = pltpu.VMEM((15, LANES, LANES), F32)
    turned = pl.pallas_call(
        turn_tile_kernel,
        out_shape=shape((15, CY, LANES), F32),
        in_specs=vmem(5),
        out_specs=vmem(1)[0],
        compiler_params=params,
        name="turn_tile",
    )(*own)
    side = pl.pallas_call(
        cut_kernel,
        out_shape=[shape((SLAB, LANES), F32)] * 2,
        in_specs=vmem(3),
        out_specs=vmem(2),
        compiler_params=params,
        name="cut_columns",
    )(turned, got_a, got_corner)
    side = swap(enumerate(side), "lateral")
    flat = pl.pallas_call(
        turn_kernel,
        out_shape=shape((15, 16 + CY, LANES), F32),
        in_specs=vmem(7),
        out_specs=vmem(1)[0],
        scratch_shapes=[fields],
        compiler_params=params,
        name="turn_fields",
    )(*own, got_a, got_b)
    band, of_own, table = tables(CX * lax.axis_size("transit"), CY * lax.axis_size("lateral"))
    held = pltpu.VMEM((HELD, LANES), F32)
    inner = pl.pallas_call(
        inner_kernel,
        out_shape=[
            shape((6, 64, 2 * LANES), F32),
            shape((12, 48, LANES), F32),
            shape((32, LANES), F32),
            shape((12, 80, LANES), F32),
            shape((80, LANES), F32),
        ],
        in_specs=vmem(9),
        out_specs=vmem(5),
        scratch_shapes=[
            pltpu.VMEM((12, HELD, LANES), F32),
            pltpu.VMEM((12, CY, 2 * LANES), BF16),
            pltpu.VMEM((6, 2 * CY, 2 * LANES), BF16),
            pltpu.VMEM((6, 112, 2 * LANES), F32),
            pltpu.VMEM((112, LANES), F32),
            pltpu.VMEM((8, HELD, LANES), F32),
            pltpu.VMEM((6, HELD, LANES), F32),
            held,
        ],
        compiler_params=params,
        cost_estimate=pl.CostEstimate(flops=800_000_000, bytes_accessed=2_000_000, transcendentals=0),
        name="inner_rows",
    )(flat, band, *of_own)
    out = pl.pallas_call(
        step_kernel,
        out_shape=[shape((6, CX, CY), F32)] * 2 + [shape((CX, CY), F32)],
        in_specs=vmem(16),
        out_specs=[pl.BlockSpec(memory_space=pltpu.HBM)] * 3,
        scratch_shapes=[
            pltpu.VMEM((15, HELD, LANES), F32),
            pltpu.VMEM((12, HELD, LANES), F32),
            pltpu.VMEM((8, HELD, LANES), F32),
            pltpu.VMEM((6, HELD, LANES), F32),
            held,
            pltpu.VMEM((6, 192, 2 * LANES), BF16),
            pltpu.VMEM((6, 192, 2 * LANES), BF16),
            pltpu.VMEM((6, 64, 2 * LANES), F32),
            pltpu.VMEM((12, CY, LANES), F32),
            pltpu.VMEM((13, CX, CY), F32),
            pltpu.SemaphoreType.DMA((13,)),
        ],
        compiler_params=params,
        name="two_steps",
    )(flat, *inner, *side[::-1], band, *table)
    return tuple(out)


def solution(mesh):
    return jax.shard_map(
        on_device,
        mesh=mesh,
        in_specs=(
            P(None, "transit", "lateral"),
            P(None, "transit", "lateral"),
            P("transit", "lateral"),
            P("transit", "lateral"),
            P("transit", "lateral"),
            P("transit", "lateral", None),
        ),
        out_specs=(
            P(None, "transit", "lateral"),
            P(None, "transit", "lateral"),
            P("transit", "lateral"),
        ),
        check_vma=False,
    )
```
